512 devices in a mesh: ctx: 32 (over y, x), img: 16 (over z, core).
Axes of the slice: x: 4, y: 8, z: 8, core: 2. Of those that a mesh axis runs over, the one named last changes fastest.
Arguments:
- text: bfloat16 [4096, 4096], P('ctx'), may hold values from -6 to 6
- input_gain: float32 [4096], replicated, may hold values from 0.5 to 2
- q_weight: bfloat16 [4096, 4096], P('ctx', 'img'), may hold values from -0.09375 to 0.09375
- kv_weight: bfloat16 [4096, 2048], P('ctx'), may hold values from -0.09375 to 0.09375
- o_weight: bfloat16 [4096, 4096], P('img', 'ctx'), may hold values from -0.5 to 0.5
- q_gain: float32 [128], replicated, may hold values from 0.5 to 12, as said below
- k_gain: float32 [128], replicated, may hold values from 0.5 to 12, as said below
- attn_gate: float32 [1], replicated, may hold values from 0.3 to 1.5
- vision: bfloat16 [32, 256, 4096], P('img', 'ctx'), may hold values from -6 to 6
- segment_ids: int32 [4096], P('ctx'), may hold values from 0 to 127, as said below
- seg_images: int32 [128, 2], replicated, may hold values from 0 to 31, as said below
- image_slot: int32 [32], replicated, may hold values from 0 to 31, each once
Outputs:
- mixed: bfloat16 [4096, 4096], P('ctx', 'img')
The draws below stay inside these ranges and needn't reach their ends.
Inputs may be any that keep to these rules, and one draw needn't show every extreme that they name: `segment_ids`: numbers never fall along the tokens; block c of 128 tokens uses numbers from c * 4 on, 1 to 4 segments a block, and some block has 4. `seg_images`: each row names 2 different images; the tokens of one block of 128 see at most 8 different images, and some block sees exactly 8. `image_slot`: A permutation. `q_gain`: Positive. `k_gain`: Positive.
All inputs are finite; a program needn't handle non-finite values.
Results may differ from the reference program's by a relative error of at most 0.022.
The reference program's roundings to bfloat16 on the way (of `hidden`, `query` and `context`) count: a program that leaves them out, or rounds other values in their place, can miss the bound.
Values may be sent and summed in bfloat16 or wider, within the bound.
A program may use at most 64 MiB of HBM per device.

```python
import math
import jax
import jax.numpy as jnp
from jax import lax

D = 4096
HEADS = 32
KVH = 8
HD = 128
TOK_DEV = 128
SEG_DEV = 4
VIS = 2
QD = 4096
TOKENS = 4096
IMAGES = 32
VT = 256
N_IMG = 16


def shared_layout(key):
    blocks = TOKENS // TOK_DEV
    key_count, key_force = jax.random.split(jax.random.fold_in(key, 7))
    counts = jax.random.randint(key_count, (blocks,), 1, SEG_DEV + 1)
    forced = jax.random.randint(key_force, (), 0, blocks)
    counts = jnp.where(jnp.arange(blocks) == forced, SEG_DEV, counts)
    return (counts, forced)


def draw_segment_ids(key, part):
    counts, forced = shared_layout(key)
    key = jax.random.fold_in(key, 11)
    blocks = TOKENS // TOK_DEV
    block_keys = jax.random.split(key, blocks)
    perms = jax.vmap(lambda single: jax.random.permutation(single, TOK_DEV - 1))(block_keys) + 1
    cuts = perms[:, :SEG_DEV - 1]
    used = jnp.arange(SEG_DEV - 1)[None, :] < counts[:, None] - 1
    cuts = jnp.where(used, cuts, TOK_DEV)
    positions = jnp.arange(TOK_DEV)
    local = jnp.sum((cuts[:, None, :] <= positions[None, :, None]).astype(jnp.int32), axis=2)
    numbers = local + jnp.arange(blocks)[:, None] * SEG_DEV
    return numbers.reshape(TOKENS).astype(jnp.int32)


def draw_seg_images(key, part):
    counts, forced = shared_layout(key)
    key = jax.random.fold_in(key, 13)
    blocks = TOKENS // TOK_DEV
    segments = blocks * SEG_DEV
    key_rows, key_force = jax.random.split(key)
    rows = jax.vmap(lambda single: jax.random.permutation(single, IMAGES)[:VIS])(jax.random.split(key_rows, segments))
    spread = jax.random.permutation(key_force, IMAGES)
    forced_rows = spread[jnp.arange(SEG_DEV * VIS) % IMAGES].reshape(SEG_DEV, VIS)
    owner = jnp.arange(segments) // SEG_DEV
    local = jnp.arange(segments) % SEG_DEV
    rows = jnp.where((owner == forced)[:, None], forced_rows[local], rows)
    return rows.astype(jnp.int32)


def draw_q_gain(key, part):
    key = jax.random.fold_in(key, 17)
    level = jax.random.uniform(key, (HD,), jnp.float32)
    return 0.5 * 5.0 ** level


def draw_k_gain(key, part):
    key = jax.random.fold_in(key, 19)
    level = jax.random.uniform(key, (HD,), jnp.float32)
    return 0.5 * 5.0 ** level


def steps_of(own_key, dims, cuts, low, largest):
    loudness = 1.0
    for dim, parts in cuts:
        steps = jax.random.uniform(jax.random.fold_in(jax.random.fold_in(own_key, 6), dim), (parts,), jnp.float32, low / len(cuts), largest / len(cuts))
        loudness = loudness * jnp.repeat(jnp.exp(steps), dims[dim] // parts).reshape((-1,) + (1,) * (len(dims) - 1 - dim))
    return loudness


def gaussian(stream_key, extent, deviation, most, cuts=(), kind=jnp.bfloat16):
    array = jax.random.normal(stream_key, extent, jnp.float32) * deviation
    if len(cuts) > 0:
        array = steps_of(stream_key, extent, cuts, -0.22, 0.18) * array
    return jnp.clip(array, min=-most, max=most).astype(kind)


def setup_inputs(seed: int = 0) -> dict:
    key_list = jax.random.split(jax.random.key(seed), 13)
    return {
        "text": gaussian(key_list[0], (TOKENS, D), 1.0, 6.0, ((0, 32),)),
        "input_gain": jnp.clip(jnp.exp(jax.random.uniform(key_list[1], (D,), jnp.float32, math.log(0.5), math.log(2.0))), 0.5, 2.0),
        "q_weight": gaussian(key_list[2], (D, QD), D ** -0.5, 0.09375, ((0, 32), (1, 16))),
        "kv_weight": gaussian(key_list[3], (D, 2 * KVH * HD), D ** -0.5, 0.09375, ((0, 32),)),
        "o_weight": gaussian(key_list[4], (QD, D), (QD // 32) ** -0.5, 0.5, ((0, 16), (1, 32))),
        "q_gain": draw_q_gain(jax.random.fold_in(key_list[12], 71), 0),
        "k_gain": draw_k_gain(jax.random.fold_in(key_list[12], 71), 0),
        "attn_gate": jnp.clip(jax.random.uniform(key_list[7], (1,), jnp.float32, 0.3, 1.5), 0.3, 1.5),
        "vision": gaussian(key_list[8], (IMAGES, VT, D), 1.0, 6.0, ((0, 16), (1, 32))),
        "segment_ids": draw_segment_ids(jax.random.fold_in(key_list[12], 71), 0),
        "seg_images": draw_seg_images(jax.random.fold_in(key_list[12], 71), 0),
        "image_slot": jax.random.permutation(key_list[11], IMAGES).astype(jnp.int32),
    }


EPS = 1e-05

def head_norm(values, gain):
    mean_sq = lax.optimization_barrier(jnp.mean(values * values, axis=-1, keepdims=True))
    return values * lax.rsqrt(mean_sq + EPS) * gain

def reference(text, input_gain, q_weight, kv_weight, o_weight, q_gain, k_gain, attn_gate, vision, segment_ids, seg_images, image_slot):
    hidden = head_norm(text.astype(jnp.float32), input_gain).astype(jnp.bfloat16)
    query = jnp.dot(hidden, q_weight, preferred_element_type=jnp.float32)
    query = head_norm(query.reshape(TOKENS, HEADS, HD), q_gain).astype(jnp.bfloat16)
    flat_vision = vision.reshape(IMAGES * VT, D)
    projected = jnp.dot(flat_vision, kv_weight, preferred_element_type=jnp.float32)
    projected = projected.reshape(IMAGES, VT, KVH, 2, HD)
    keys = head_norm(projected[:, :, :, 0], k_gain).astype(jnp.bfloat16)
    values = projected[:, :, :, 1].astype(jnp.bfloat16)
    slots = jnp.take(image_slot, jnp.take(seg_images, segment_ids, axis=0), axis=0).astype(jnp.int32)
    nblocks = TOKENS // TOK_DEV
    group = HEADS // KVH
    scale = HD ** (-0.5)

    def one_block(index):
        block = index // KVH
        head = index % KVH
        start = (block * TOK_DEV).astype(jnp.int32)
        q_block = lax.dynamic_slice_in_dim(query, start, TOK_DEV, 0)
        q_block = lax.dynamic_slice_in_dim(q_block, (head * group).astype(jnp.int32), group, 1).astype(jnp.float32)
        s_block = lax.dynamic_slice_in_dim(slots, start, TOK_DEV, 0)
        k_head = lax.dynamic_index_in_dim(keys, head, 2, keepdims=False)
        v_head = lax.dynamic_index_in_dim(values, head, 2, keepdims=False)
        k_sel = jnp.take(k_head, s_block, axis=0).reshape(TOK_DEV, VIS * VT, HD).astype(jnp.float32)
        v_sel = jnp.take(v_head, s_block, axis=0).reshape(TOK_DEV, VIS * VT, HD).astype(jnp.float32)
        scores = jnp.einsum('tgd,tkd->tgk', q_block, k_sel) * scale
        top = lax.optimization_barrier(jnp.max(scores, axis=-1, keepdims=True))
        weights = jnp.exp(scores - top)
        total = lax.optimization_barrier(jnp.sum(weights, axis=-1))
        rounded = lax.optimization_barrier(weights.astype(jnp.bfloat16)).astype(jnp.float32)
        context = jnp.einsum('tgk,tkd->tgd', rounded, v_sel) / total[..., None]
        return context.astype(jnp.bfloat16)
    outs = lax.map(one_block, jnp.arange(nblocks * KVH, dtype=jnp.int32))
    context = outs.reshape(nblocks, KVH, TOK_DEV, group, HD).transpose(0, 2, 1, 3, 4).reshape(TOKENS, QD)
    width_group = QD // N_IMG

    def add_group(index, total):
        part_context = lax.dynamic_slice_in_dim(context, index * width_group, width_group, 1)
        part_weight = lax.dynamic_slice_in_dim(o_weight, index * width_group, width_group, 0)
        part = jnp.dot(part_context, part_weight, preferred_element_type=jnp.float32).astype(jnp.bfloat16)
        return total + lax.optimization_barrier(part).astype(jnp.float32)
    update = lax.fori_loop(0, N_IMG, add_group, jnp.zeros((TOKENS, D), jnp.float32))
    return (text.astype(jnp.float32) + jnp.tanh(attn_gate[0]) * update).astype(jnp.bfloat16)
```

```python
import functools

import jax
import jax.numpy as jnp
from jax import lax
from jax.experimental import pallas as pl
from jax.experimental.pallas import tpu as pltpu
from jax.sharding import PartitionSpec as P

MESH = pl.DeviceIdType.MESH
EPS = 1e-05
NEG = -1e30
F32 = jnp.float32
BF16 = jnp.bfloat16
NX, NY, NZ = 4, 8, 8
COPIES = 192


def kernel(
    text_ref, in_gain_ref, qw_ref, kvw_ref, ow_ref, q_gain_ref, k_gain_ref, gate_ref, vis_ref,
    seg_ref, seg_img_ref, slot_ref, out_ref,
    text, hid, hid_in, vis, wkv, wq, wo, wo_other, part, part_in, kv_rows, stage, kv_all, ctx, upd, upd_in,
    send_sem, recv_sem, local_sem,
):
    c = lax.axis_index("ctx")
    i = lax.axis_index("img")
    x, y, z, k = lax.rem(c, NX), c // NX, i // 2, lax.rem(i, 2)
    wrap = lambda a, n: lax.rem(a + 2 * n, n)
    at = lambda xx, yy, zz, kk: (yy * NX + xx, zz * 2 + kk)
    to_x = lambda d: at(wrap(x + d, NX), y, z, k)
    to_y = lambda d: at(x, wrap(y + d, NY), z, k)
    to_z = lambda d: at(x, y, wrap(z + d, NZ), k)
    other = at(x, y, z, 1 - k)
    sent = []

    def send(src, dst, device):
        n = len(sent)
        copy = pltpu.make_async_remote_copy(
            src_ref=src, dst_ref=dst, send_sem=send_sem.at[n], recv_sem=recv_sem.at[n],
            device_id=device, device_id_type=MESH,
        )
        copy.start()
        sent.append(copy)
        return copy

    barrier = pltpu.get_barrier_semaphore()
    peers = [to_x(d) for d in (1, 2, 3)] + [to_y(d) for d in range(1, NY)]
    peers += [to_z(d) for d in range(1, NZ)] + [other]
    for peer in peers:
        pl.semaphore_signal(barrier, inc=1, device_id=peer, device_id_type=MESH)
    local = []

    def fetch(src, dst):
        copy = pltpu.make_async_copy(src, dst, local_sem.at[len(local)])
        copy.start()
        local.append(copy)
        return copy

    get_text = fetch(text_ref, text)
    get_own = [
        fetch(vis_ref.at[:, pl.ds(0, 2048)], vis.at[z, k, 0]),
        fetch(vis_ref.at[:, pl.ds(2048, 2048)], vis.at[z, k, 1]),
        fetch(kvw_ref.at[:, pl.ds(pl.multiple_of(z * 256 + k * 128, 128), 128)], wkv.at[c]),
        fetch(qw_ref, wq.at[y]),
        fetch(ow_ref, wo.at[c]),
    ]
    get_text.wait()

    @pl.loop(0, 8)
    def _(block):
        rows = pl.ds(pl.multiple_of(block * 16, 16), 16)
        values = text[rows, :].astype(F32)
        mean_sq = jnp.mean(values * values, axis=-1, keepdims=True)
        values = (values * lax.rsqrt(mean_sq + EPS) * in_gain_ref[...]).astype(BF16)
        for b in range(32):
            hid[b % NX, b // NX // 4, b // NX % 4, rows, :] = values[:, b * 128:(b + 1) * 128]

    for copy in get_own:
        copy.wait()
    pl.semaphore_wait(barrier, len(peers))

    vis_p, vis_m, vis_o = {}, {}, []
    for h in (0, 1):
        vis_p[1, h] = send(vis.at[z, k, h], vis.at[z, k, h], to_z(1))
        vis_m[1, h] = send(vis.at[z, k, h], vis.at[z, k, h], to_z(-1))
    kv_y = {d: send(wkv.at[c], wkv.at[c], to_y(d)) for d in (1, -1, 2, -2, 3, -3, 4)}
    kv_x = [send(wkv.at[c], wkv.at[c], to_x(d)) for d in (1, -1, 2)]
    for h in (0, 1):
        vis_o.append(send(vis.at[z, k, h], vis.at[z, k, h], other))
    q_p, q_m = {}, {}
    q_p[1] = send(wq.at[y], wq.at[y], to_y(1))
    q_m[1] = send(wq.at[y], wq.at[y], to_y(-1))
    hid_x = {}
    for d in (1, 3, 2):
        hid_x[d] = send(hid.at[wrap(x + d, NX), k], hid_in.at[d - 1, k], to_x(d))
    o_xp = send(wo.at[c], wo.at[c], to_x(1))
    o_xm = send(wo.at[c], wo.at[c], to_x(-1))

    def vis_step(s):
        for h in (0, 1):
            for ring, sign in ((vis_p, 1), (vis_m, -1)):
                if (s, h) not in ring:
                    continue
                ring[s, h].wait_recv()
                block = vis.at[wrap(z - sign * s, NZ), k, h]
                if s < 3 or (s == 3 and h == (0 if sign == 1 else 1)):
                    ring[s + 1, h] = send(block, block, to_z(sign))
                vis_o.append(send(block, block, other))

    def kv_step(s):
        for d in ((s, -s) if s < 4 else (4,)):
            kv_y[d].wait_recv()
            block = wkv.at[wrap(y - d, NY) * NX + x]
            for e in (1, -1, 2):
                kv_x.append(send(block, block, to_x(e)))

    def q_step(s):
        for ring, sign in ((q_p, 1), (q_m, -1)):
            ring[s].wait_recv()
            block = wq.at[wrap(y - sign * s, NY)]
            if s == 3:
                block = block.at[pl.ds(0 if sign == 1 else 64, 64)]
            if s < 4:
                ring[s + 1] = send(block, block, to_y(sign))

    o_p, o_m = {}, {}

    def o_bundle(yy, first=0, count=NX):
        return wo.at[pl.ds(yy * NX + first, count)]

    def o_step(s):
        for ring, sign in ((o_p, 1), (o_m, -1)):
            ring[s].wait_recv()
            yy = wrap(y - sign * s, NY)
            block = o_bundle(yy)
            if s == 3:
                block = o_bundle(yy, 0 if sign == 1 else 2, 2)
            if s < 4:
                ring[s + 1] = send(block, block, to_y(sign))
                o_share(yy)
        if s == 4:
            o_share(wrap(y + 4, NY))

    o_o = []

    def o_share(yy):
        o_o.append(send(wo.at[pl.ds(yy * NX + 2 * (1 - k), 2)], wo_other.at[yy], other))

    vis_step(1)
    kv_step(1)
    vis_step(2)
    kv_step(2)
    q_step(1)
    o_xp.wait_recv()
    o_xm.wait_recv()
    half = wo.at[y * NX + wrap(x - 1, NX), pl.ds(0, 128)]
    o_x2p = send(half, half, to_x(1))
    half = wo.at[y * NX + wrap(x + 1, NX), pl.ds(128, 128)]
    o_x2m = send(half, half, to_x(-1))
    kv_step(3)
    kv_step(4)
    vis_step(3)
    q_step(2)
    hid_o = {}
    for d in (1, 3, 2):
        hid_x[d].wait_recv()
        hid_o[d] = send(hid_in.at[d - 1, k], hid_in.at[d - 1, k], other)
    vis_step(4)
    q_step(3)
    for copy in kv_x:
        copy.wait_recv()
    for copy in vis_o:
        copy.wait_recv()

    rows = jnp.zeros((256, 128), F32)
    for h in (0, 1):
        rows += jnp.dot(
            vis[:, :, h].reshape(256, 2048), wkv[16 * h:16 * (h + 1)].reshape(2048, 128),
            preferred_element_type=F32,
        )
    mean_sq = jnp.mean(rows * rows, axis=-1, keepdims=True)
    normed = rows * lax.rsqrt(mean_sq + EPS) * k_gain_ref[...]
    kv_rows[...] = jnp.where(k == 0, normed, rows).reshape(32, 8, 128)

    offsets = [(dx, dy) for dy in (0, 4, 3, 5, 2, 6, 1, 7) for dx in (2, 1, 3, 0)]

    def pick(block):
        tiles = []
        for s in range(8):
            slot = slot_ref[seg_img_ref[block * 8 + s]]
            tiles.append(kv_rows[slot])
        return jnp.concatenate(tiles, axis=0).astype(BF16)

    kv_a = {}
    kv_all[k, 0] = pick(c)
    for dx, dy in offsets:
        if (dx, dy) == (0, 0):
            continue
        n = dy * NX + dx
        xx, yy = wrap(x + dx, NX), wrap(y + dy, NY)
        stage[n] = pick(yy * NX + xx)
        kv_a[n] = send(stage.at[n], kv_all.at[k, n], at(xx, yy, z, k))

    o_x2p.wait_recv()
    o_x2m.wait_recv()
    o_p[1] = send(o_bundle(y), o_bundle(y), to_y(1))
    o_m[1] = send(o_bundle(y), o_bundle(y), to_y(-1))
    o_share(y)
    q_step(4)
    for copy in hid_o.values():
        copy.wait_recv()
    wq_all = wq[...].reshape(1024, 256)
    part_x = {}
    query = None
    for d in (1, 3, 2, 0):
        blocks = [
            (hid[x, b // 4, b % 4] if d == 0 else hid_in[d - 1, b // 4, b % 4]) for b in range(8)
        ]
        product = jnp.dot(jnp.concatenate(blocks, axis=1), wq_all, preferred_element_type=F32)
        if d == 0:
            query = product
        else:
            part[d - 1] = product.astype(BF16)
            part_x[d] = send(part.at[d - 1], part_in.at[d - 1], to_x(-d))
    o_step(1)
    for d in (1, 3, 2):
        part_x[d].wait_recv()
        query += part_in[d - 1].astype(F32)
    heads = []
    for n in (0, 1):
        head = query[:, 128 * n:128 * (n + 1)]
        mean_sq = jnp.mean(head * head, axis=-1, keepdims=True)
        heads.append((head * lax.rsqrt(mean_sq + EPS) * q_gain_ref[...]).astype(BF16))

    kv_o = []
    for dy in (1, 7, 2, 6, 3, 5, 4, 0):
        for dx in range(NX):
            if (dx, dy) != (0, 0):
                kv_a[dy * NX + dx].wait_recv()
        block = kv_all.at[k, pl.ds(dy * NX, NX)]
        kv_o.append(send(block, block, other))
    o_step(2)
    for copy in kv_o:
        copy.wait_recv()

    keys = kv_all[0].reshape(2048, 128)
    values = kv_all[1].reshape(2048, 128)
    column = lax.broadcasted_iota(jnp.int32, (128, 2048), 1)
    live = lax.rem(column, 64) // 16 == seg_ref[...] - 4 * c
    for n in (0, 1):
        scores = lax.dot_general(
            heads[n], keys, (((1,), (1,)), ((), ())), preferred_element_type=F32
        ) * (128 ** -0.5)
        scores = jnp.where(live, scores, NEG)
        weights = jnp.exp(scores - jnp.max(scores, axis=-1, keepdims=True))
        total = jnp.sum(weights, axis=-1, keepdims=True)
        acc = jnp.dot(weights.astype(BF16), values, preferred_element_type=F32)
        ctx[k, :, 128 * n:128 * (n + 1)] = (acc / total).astype(BF16)
    ctx_o = send(ctx.at[k], ctx.at[k], other)
    o_step(3)
    o_step(4)
    for copy in o_o:
        copy.wait_recv()
    ctx_o.wait_recv()

    upd_z = {}
    mine, theirs = ctx[k], ctx[1 - k]
    update = None
    for d in (4, 3, 5, 2, 6, 1, 7, 0):
        zz = wrap(z + d, NZ)
        own_w = jnp.concatenate([wo[zz * NX + 2 * k + e] for e in (0, 1)], axis=1)
        other_w = jnp.concatenate([wo_other[zz, e] for e in (0, 1)], axis=1)
        product = jnp.dot(mine, own_w, preferred_element_type=F32)
        product += jnp.dot(theirs, other_w, preferred_element_type=F32)
        if d == 0:
            update = product.astype(BF16).astype(F32)
        else:
            upd[d - 1] = product.astype(BF16)
            upd_z[d] = send(upd.at[d - 1], upd_in.at[d - 1], to_z(d))
    for d in (1, 7, 2, 6, 3, 5, 4):
        upd_z[d].wait_recv()
        update += upd_in[d - 1].astype(F32)
    own_text = text[:, pl.ds(pl.multiple_of(i * 256, 256), 256)].astype(F32)
    gate = jnp.tanh(jnp.full((1, 256), gate_ref[0], F32))
    out_ref[...] = (own_text + gate * update).astype(BF16)
    for copy in sent:
        copy.wait_send()


def body(
    text, input_gain, q_weight, kv_weight, o_weight, q_gain, k_gain, attn_gate, vision, segment_ids,
    seg_images, image_slot,
):
    vmem = pl.BlockSpec(memory_space=pltpu.VMEM)
    smem = pl.BlockSpec(memory_space=pltpu.SMEM)
    hbm = pl.BlockSpec(memory_space=pl.ANY)
    return pl.pallas_call(
        kernel,
        out_shape=jax.ShapeDtypeStruct((128, 256), BF16),
        in_specs=[hbm, vmem, hbm, hbm, hbm, vmem, vmem, smem, hbm, vmem, smem, smem],
        out_specs=vmem,
        scratch_shapes=[
            pltpu.VMEM((128, 4096), BF16),
            pltpu.VMEM((4, 2, 4, 128, 128), BF16),
            pltpu.VMEM((3, 2, 4, 128, 128), BF16),
            pltpu.VMEM((8, 2, 2, 16, 2048), BF16),
            pltpu.VMEM((32, 128, 128), BF16),
            pltpu.VMEM((8, 128, 256), BF16),
            pltpu.VMEM((32, 256, 128), BF16),
            pltpu.VMEM((8, 2, 256, 128), BF16),
            pltpu.VMEM((3, 128, 256), BF16),
            pltpu.VMEM((3, 128, 256), BF16),
            pltpu.VMEM((32, 8, 128), F32),
            pltpu.VMEM((32, 64, 128), BF16),
            pltpu.VMEM((2, 32, 64, 128), BF16),
            pltpu.VMEM((2, 128, 256), BF16),
            pltpu.VMEM((7, 128, 256), BF16),
            pltpu.VMEM((7, 128, 256), BF16),
            pltpu.SemaphoreType.DMA((COPIES,)),
            pltpu.SemaphoreType.DMA((COPIES,)),
            pltpu.SemaphoreType.DMA((8,)),
        ],
        compiler_params=pltpu.CompilerParams(
            collective_id=0, has_side_effects=True, vmem_limit_bytes=48 * 2**20
        ),
        cost_estimate=pl.CostEstimate(flops=2 * 10**9, bytes_accessed=4 * 10**6, transcendentals=600000),
    )(
        text, input_gain.reshape(1, -1), q_weight, kv_weight, o_weight, q_gain.reshape(1, -1),
        k_gain.reshape(1, -1), attn_gate, vision.reshape(16, 4096), segment_ids.reshape(-1, 1),
        seg_images.reshape(-1), image_slot,
    )


def solution(mesh):
    return jax.shard_map(
        body,
        mesh=mesh,
        in_specs=(
            P("ctx", None), P(), P("ctx", "img"), P("ctx", None), P("img", "ctx"), P(), P(), P(),
            P("img", "ctx", None), P("ctx"), P(), P(),
        ),
        out_specs=P("ctx", "img"),
        check_vma=False,
    )
```

```python
import functools

import jax
import jax.numpy as jnp
from jax import lax
from jax.experimental import pallas as pl
from jax.experimental.pallas import tpu as pltpu
from jax.sharding import PartitionSpec as P

MESH = pl.DeviceIdType.MESH
EPS = 1e-05
NEG = -1e30
F32 = jnp.float32
BF16 = jnp.bfloat16
NX, NY, NZ = 4, 8, 8
COPIES = 192


def kernel(
    text_ref, in_gain_hbm, qw_ref, kvw_ref, ow_ref, q_gain_hbm, k_gain_hbm, gate_ref, vis_ref,
    seg_hbm, seg_img_hbm, slot_hbm, out_ref,
    in_gain_ref, q_gain_ref, k_gain_ref, seg_ref, seg_img_ref, slot_ref, text, hid, hid_in, vis, wkv, wq, woa, wob, woa_other, wob_other, part, part_in, kv_rows, stage, kv_all, ctx, upd, upd_in,
    send_sem, recv_sem, local_sem,
):
    c = lax.axis_index("ctx")
    i = lax.axis_index("img")
    x, y, z, k = lax.rem(c, NX), c // NX, i // 2, lax.rem(i, 2)
    wrap = lambda a, n: lax.rem(a + 2 * n, n)
    at = lambda xx, yy, zz, kk: (yy * NX + xx, zz * 2 + kk)
    to_x = lambda d: at(wrap(x + d, NX), y, z, k)
    to_y = lambda d: at(x, wrap(y + d, NY), z, k)
    to_z = lambda d: at(x, y, wrap(z + d, NZ), k)
    other = at(x, y, z, 1 - k)
    sent = []

    def send(src, dst, device):
        n = len(sent)
        copy = pltpu.make_async_remote_copy(
            src_ref=src, dst_ref=dst, send_sem=send_sem.at[n], recv_sem=recv_sem.at[n],
            device_id=device, device_id_type=MESH,
        )
        copy.start()
        sent.append(copy)
        return copy

    barrier = pltpu.get_barrier_semaphore()
    peers = [to_x(d) for d in (1, 2, 3)] + [to_y(d) for d in range(1, NY)]
    peers += [to_z(d) for d in range(1, NZ)] + [other]
    for peer in peers:
        pl.semaphore_signal(barrier, inc=1, device_id=peer, device_id_type=MESH)
    local = []

    def fetch(src, dst):
        copy = pltpu.make_async_copy(src, dst, local_sem.at[len(local)])
        copy.start()
        local.append(copy)
        return copy

    get_text = [fetch(text_ref, text), fetch(in_gain_hbm, in_gain_ref)]
    get_vis = [fetch(vis_ref.at[:, pl.ds(1024 * h, 1024)], vis.at[z, k, h]) for h in range(4)]
    get_own = [
        fetch(kvw_ref.at[:, pl.ds(pl.multiple_of(z * 256 + k * 128, 128), 128)], wkv.at[c]),
        fetch(qw_ref, wq.at[y]),
        fetch(ow_ref.at[pl.ds(0, 128)], woa.at[x, y]),
        fetch(ow_ref.at[pl.ds(128, 128)], wob.at[y, x]),
        fetch(q_gain_hbm, q_gain_ref),
        fetch(k_gain_hbm, k_gain_ref),
        fetch(seg_hbm, seg_ref),
        fetch(seg_img_hbm, seg_img_ref),
        fetch(slot_hbm, slot_ref),
    ]
    for copy in get_text:
        copy.wait()

    @pl.loop(0, 8)
    def _(block):
        rows = pl.ds(pl.multiple_of(block * 16, 16), 16)
        values = text[rows, :].astype(F32)
        mean_sq = jnp.mean(values * values, axis=-1, keepdims=True)
        values = (values * lax.rsqrt(mean_sq + EPS) * in_gain_ref[...]).astype(BF16)
        for b in range(32):
            hid[b % NX, b // NX // 4, b // NX % 4, rows, :] = values[:, b * 128:(b + 1) * 128]

    for copy in get_vis + get_own:
        copy.wait()
    pl.semaphore_wait(barrier, len(peers))

    vis_p, vis_m, vis_o = {}, {}, []
    for h in range(4):
        vis_p[1, h] = send(vis.at[z, k, h], vis.at[z, k, h], to_z(1))
        vis_m[1, h] = send(vis.at[z, k, h], vis.at[z, k, h], to_z(-1))
    kv_y = {d: send(wkv.at[c], wkv.at[c], to_y(d)) for d in (1, -1, 2, -2, 3, -3, 4)}
    kv_x = [send(wkv.at[c], wkv.at[c], to_x(d)) for d in (1, -1, 2)]
    vis_o.append(send(vis.at[z, k], vis.at[z, k], other))
    q_p, q_m = {}, {}
    q_p[1] = send(wq.at[y], wq.at[y], to_y(1))
    q_m[1] = send(wq.at[y], wq.at[y], to_y(-1))
    hid_x = {}
    a_p, a_m, b_p, b_m = {}, {}, {}, {}
    a_p[1] = send(woa.at[x, y], woa.at[x, y], to_y(1))
    a_m[1] = send(woa.at[x, y], woa.at[x, y], to_y(-1))
    b_xp = send(wob.at[y, x], wob.at[y, x], to_x(1))
    b_xm = send(wob.at[y, x], wob.at[y, x], to_x(-1))

    def vis_step(s):
        for h in (0, 2, 1, 3):
            for ring, sign in ((vis_p, 1), (vis_m, -1)):
                if (s, h) not in ring:
                    continue
                ring[s, h].wait_recv()
                if s < 3 or (s == 3 and (h < 2) == (sign == 1)):
                    block = vis.at[wrap(z - sign * s, NZ), k, h]
                    ring[s + 1, h] = send(block, block, to_z(sign))
        for sign in ((1, -1) if s < 4 else (1,)):
            block = vis.at[wrap(z - sign * s, NZ), k]
            vis_o.append(send(block, block, other))

    def kv_step(s):
        for d in ((s, -s) if s < 4 else (4,)):
            kv_y[d].wait_recv()
            block = wkv.at[wrap(y - d, NY) * NX + x]
            for e in (1, -1, 2):
                kv_x.append(send(block, block, to_x(e)))

    def row_step(p, m, s, block, half):
        for ring, sign in ((p, 1), (m, -1)):
            ring[s].wait_recv()
            yy = wrap(y - sign * s, NY)
            if s < 4:
                piece = half(yy, 0 if sign == 1 else 1) if s == 3 else block(yy)
                ring[s + 1] = send(piece, piece, to_y(sign))

    def q_step(s):
        row_step(q_p, q_m, s, lambda yy: wq.at[yy], lambda yy, n: wq.at[yy, pl.ds(64 * n, 64)])

    def a_step(s):
        row_step(
            a_p, a_m, s, lambda yy: woa.at[x, yy], lambda yy, n: woa.at[x, yy, pl.ds(64 * n, 64)]
        )

    o_o = []

    def b_share(yy):
        o_o.append(send(wob.at[yy, pl.ds(2 * (1 - k), 2)], wob_other.at[yy], other))

    def b_step(s):
        row_step(b_p, b_m, s, lambda yy: wob.at[yy], lambda yy, n: wob.at[yy, pl.ds(2 * n, 2)])
        for d in ((s, -s) if s < 4 else (4,)):
            b_share(wrap(y - d, NY))

    vis_step(1)
    b_xp.wait_recv()
    b_xm.wait_recv()
    half = wob.at[y, wrap(x - 1, NX), pl.ds(0, 64)]
    b_x2p = send(half, half, to_x(1))
    half = wob.at[y, wrap(x + 1, NX), pl.ds(64, 64)]
    b_x2m = send(half, half, to_x(-1))
    kv_step(1)
    q_step(1)
    a_step(1)
    vis_step(2)
    kv_step(2)
    b_x2p.wait_recv()
    b_x2m.wait_recv()
    b_p[1] = send(wob.at[y], wob.at[y], to_y(1))
    b_m[1] = send(wob.at[y], wob.at[y], to_y(-1))
    b_share(y)
    kv_step(3)
    kv_step(4)
    q_step(2)
    a_step(2)
    vis_step(3)
    for d in (1, 3, 2):
        hid_x[d] = send(hid.at[wrap(x + d, NX), k], hid_in.at[d - 1, k], to_x(d))
    b_step(1)
    q_step(3)
    a_step(3)
    vis_step(4)
    for copy in kv_x:
        copy.wait_recv()
    for copy in vis_o:
        copy.wait_recv()

    rows = jnp.zeros((256, 128), F32)
    for h in range(4):
        rows += jnp.dot(
            vis[:, :, h].reshape(256, 1024), wkv[8 * h:8 * (h + 1)].reshape(1024, 128),
            preferred_element_type=F32,
        )
    mean_sq = jnp.mean(rows * rows, axis=-1, keepdims=True)
    normed = rows * lax.rsqrt(mean_sq + EPS) * k_gain_ref[...]
    kv_rows[...] = jnp.where(k == 0, normed, rows).reshape(32, 8, 128)

    offsets = [(dx, dy) for dy in (0, 4, 3, 5, 2, 6, 1, 7) for dx in (2, 1, 3, 0)]

    def pick(block):
        tiles = []
        for s in range(8):
            slot = slot_ref[0, seg_img_ref[s % 2, block * 4 + s // 2]]
            tiles.append(kv_rows[slot])
        return jnp.concatenate(tiles, axis=0).astype(BF16)

    kv_a = {}
    kv_all[k, 0] = pick(c)
    for dx, dy in offsets:
        if (dx, dy) == (0, 0):
            continue
        n = dy * NX + dx
        xx, yy = wrap(x + dx, NX), wrap(y + dy, NY)
        stage[n] = pick(yy * NX + xx)
        kv_a[n] = send(stage.at[n], kv_all.at[k, n], at(xx, yy, z, k))

    b_step(2)
    a_step(4)
    a_x = {d: send(woa.at[x], woa.at[x], to_x(d)) for d in (1, -1)}
    hid_o = {}
    for d in (1, 3, 2):
        hid_x[d].wait_recv()
        hid_o[d] = send(hid_in.at[d - 1, k], hid_in.at[d - 1, k], other)
    q_step(4)
    for copy in hid_o.values():
        copy.wait_recv()
    wq_all = wq[...].reshape(1024, 256)
    part_x = {}
    query = None
    for d in (1, 3, 2, 0):
        blocks = [
            (hid[x, b // 4, b % 4] if d == 0 else hid_in[d - 1, b // 4, b % 4]) for b in range(8)
        ]
        product = jnp.dot(jnp.concatenate(blocks, axis=1), wq_all, preferred_element_type=F32)
        if d == 0:
            query = product
        else:
            part[d - 1] = product.astype(BF16)
            part_x[d] = send(part.at[d - 1], part_in.at[d - 1], to_x(-d))
    b_step(3)
    for d in (1, 3, 2):
        part_x[d].wait_recv()
        query += part_in[d - 1].astype(F32)
    heads = []
    for n in (0, 1):
        head = query[:, 128 * n:128 * (n + 1)]
        mean_sq = jnp.mean(head * head, axis=-1, keepdims=True)
        heads.append((head * lax.rsqrt(mean_sq + EPS) * q_gain_ref[...]).astype(BF16))

    for d in (1, -1):
        a_x[d].wait_recv()
    a_x2 = {}
    for d in (1, -1):
        piece = woa.at[wrap(x - d, NX), pl.ds(0 if d == 1 else 4, 4)]
        a_x2[d] = send(piece, piece, to_x(d))
    b_step(4)
    kv_o = []
    for dy in (1, 7, 2, 6, 3, 5, 4, 0):
        for dx in range(NX):
            if (dx, dy) != (0, 0):
                kv_a[dy * NX + dx].wait_recv()
        block = kv_all.at[k, pl.ds(dy * NX, NX)]
        kv_o.append(send(block, block, other))
    for copy in kv_o:
        copy.wait_recv()

    keys = kv_all[0].reshape(2048, 128)
    values = kv_all[1].reshape(2048, 128)
    column = lax.broadcasted_iota(jnp.int32, (128, 2048), 1)
    segment = jnp.transpose(jnp.broadcast_to((seg_ref[...] - 4 * c).astype(F32), (128, 128)))
    live = (lax.rem(column, 64) // 16).astype(F32) == segment[:, :1]
    for n in (0, 1):
        scores = lax.dot_general(
            heads[n], keys, (((1,), (1,)), ((), ())), preferred_element_type=F32
        ) * (128 ** -0.5)
        scores = jnp.where(live, scores, NEG)
        weights = jnp.exp(scores - jnp.max(scores, axis=-1, keepdims=True))
        total = jnp.sum(weights, axis=-1, keepdims=True)
        acc = jnp.dot(weights.astype(BF16), values, preferred_element_type=F32)
        ctx[k, :, 128 * n:128 * (n + 1)] = (acc / total).astype(BF16)
    ctx_o = send(ctx.at[k], ctx.at[k], other)
    for d in (1, -1):
        a_x2[d].wait_recv()
    for e in (0, 1):
        o_o.append(send(woa.at[2 * (1 - k) + e], woa_other.at[e], other))
    for copy in o_o:
        copy.wait_recv()
    ctx_o.wait_recv()

    upd_z = {}
    mine, theirs = ctx[k], ctx[1 - k]
    update = None
    for d in (4, 3, 5, 2, 6, 1, 7, 0):
        zz = wrap(z + d, NZ)
        own_a = jnp.concatenate([woa[2 * k + e, zz] for e in (0, 1)], axis=1)
        own_b = jnp.concatenate([wob[zz, 2 * k + e] for e in (0, 1)], axis=1)
        own_w = jnp.concatenate([own_a, own_b], axis=0)
        other_a = jnp.concatenate([woa_other[e, zz] for e in (0, 1)], axis=1)
        other_b = jnp.concatenate([wob_other[zz, e] for e in (0, 1)], axis=1)
        other_w = jnp.concatenate([other_a, other_b], axis=0)
        product = jnp.dot(mine, own_w, preferred_element_type=F32)
        product += jnp.dot(theirs, other_w, preferred_element_type=F32)
        if d == 0:
            update = product.astype(BF16).astype(F32)
        else:
            upd[d - 1] = product.astype(BF16)
            upd_z[d] = send(upd.at[d - 1], upd_in.at[d - 1], to_z(d))
    for d in (1, 7, 2, 6, 3, 5, 4):
        upd_z[d].wait_recv()
        update += upd_in[d - 1].astype(F32)
    own_text = text[:, pl.ds(pl.multiple_of(i * 256, 256), 256)].astype(F32)
    gate = jnp.tanh(jnp.full((1, 256), gate_ref[0], F32))
    out_ref[...] = (own_text + gate * update).astype(BF16)
    for copy in sent:
        copy.wait_send()


def body(
    text, input_gain, q_weight, kv_weight, o_weight, q_gain, k_gain, attn_gate, vision, segment_ids,
    seg_images, image_slot,
):
    vmem = pl.BlockSpec(memory_space=pltpu.VMEM)
    smem = pl.BlockSpec(memory_space=pltpu.SMEM)
    hbm = pl.BlockSpec(memory_space=pltpu.HBM)
    return pl.pallas_call(
        kernel,
        out_shape=jax.ShapeDtypeStruct((128, 256), BF16),
        in_specs=[hbm] * 7 + [smem] + [hbm] * 4,
        out_specs=vmem,
        scratch_shapes=[
            pltpu.VMEM((1, 4096), F32),
            pltpu.VMEM((1, 128), F32),
            pltpu.VMEM((1, 128), F32),
            pltpu.VMEM((1, 128), jnp.int32),
            pltpu.SMEM((2, 128), jnp.int32),
            pltpu.SMEM((1, 32), jnp.int32),
            pltpu.VMEM((128, 4096), BF16),
            pltpu.VMEM((4, 2, 4, 128, 128), BF16),
            pltpu.VMEM((3, 2, 4, 128, 128), BF16),
            pltpu.VMEM((8, 2, 4, 16, 1024), BF16),
            pltpu.VMEM((32, 128, 128), BF16),
            pltpu.VMEM((8, 128, 256), BF16),
            pltpu.VMEM((4, 8, 128, 128), BF16),
            pltpu.VMEM((8, 4, 128, 128), BF16),
            pltpu.VMEM((2, 8, 128, 128), BF16),
            pltpu.VMEM((8, 2, 128, 128), BF16),
            pltpu.VMEM((3, 128, 256), BF16),
            pltpu.VMEM((3, 128, 256), BF16),
            pltpu.VMEM((32, 8, 128), F32),
            pltpu.VMEM((32, 64, 128), BF16),
            pltpu.VMEM((2, 32, 64, 128), BF16),
            pltpu.VMEM((2, 128, 256), BF16),
            pltpu.VMEM((7, 128, 256), BF16),
            pltpu.VMEM((7, 128, 256), BF16),
            pltpu.SemaphoreType.DMA((COPIES,)),
            pltpu.SemaphoreType.DMA((COPIES,)),
            pltpu.SemaphoreType.DMA((32,)),
        ],
        compiler_params=pltpu.CompilerParams(
            collective_id=0, has_side_effects=True, vmem_limit_bytes=67 * 10**6
        ),
        cost_estimate=pl.CostEstimate(flops=2 * 10**9, bytes_accessed=4 * 10**6, transcendentals=600000),
    )(
        text, input_gain.reshape(1, -1), q_weight, kv_weight, o_weight, q_gain.reshape(1, -1),
        k_gain.reshape(1, -1), attn_gate, vision.reshape(16, 4096), segment_ids.reshape(1, -1),
        seg_images.T, image_slot.reshape(1, -1),
    )


def solution(mesh):
    return jax.shard_map(
        body,
        mesh=mesh,
        in_specs=(
            P("ctx", None), P(), P("ctx", "img"), P("ctx", None), P("img", "ctx"), P(), P(), P(),
            P("img", "ctx", None), P("ctx"), P(), P(),
        ),
        out_specs=P("ctx", "img"),
        check_vma=False,
    )
```

```python
import functools

import jax
import jax.numpy as jnp
from jax import lax
from jax.experimental import pallas as pl
from jax.experimental.pallas import tpu as pltpu
from jax.sharding import PartitionSpec as P

MESH = pl.DeviceIdType.MESH
EPS = 1e-05
NEG = -1e30
F32 = jnp.float32
BF16 = jnp.bfloat16
NX, NY, NZ = 4, 8, 8
COPIES = 192


def kernel(
    text_ref, in_gain_hbm, qw_ref, kvw_ref, ow_ref, q_gain_hbm, k_gain_hbm, gate_ref, vis_ref,
    seg_hbm, seg_img_hbm, slot_hbm, out_ref,
    in_gain_ref, q_gain_ref, k_gain_ref, seg_ref, seg_img_ref, slot_ref, text, hid, hid_in, vis, wkv, wq, woa, wob, woa_other, wob_other, part, part_in, kv_rows, stage, kv_all, ctx, upd, upd_in,
    send_sem, recv_sem, local_sem,
):
    c = lax.axis_index("ctx")
    i = lax.axis_index("img")
    x, y, z, k = lax.rem(c, NX), c // NX, i // 2, lax.rem(i, 2)
    wrap = lambda a, n: lax.rem(a + 2 * n, n)
    at = lambda xx, yy, zz, kk: (yy * NX + xx, zz * 2 + kk)
    to_x = lambda d: at(wrap(x + d, NX), y, z, k)
    to_y = lambda d: at(x, wrap(y + d, NY), z, k)
    to_z = lambda d: at(x, y, wrap(z + d, NZ), k)
    other = at(x, y, z, 1 - k)
    sent = []

    def send(src, dst, device):
        n = len(sent)
        copy = pltpu.make_async_remote_copy(
            src_ref=src, dst_ref=dst, send_sem=send_sem.at[n], recv_sem=recv_sem.at[n],
            device_id=device, device_id_type=MESH,
        )
        copy.start()
        sent.append(copy)
        return copy

    barrier = pltpu.get_barrier_semaphore()
    peers = [to_x(d) for d in (1, 2, 3)] + [to_y(d) for d in range(1, NY)]
    peers += [to_z(d) for d in range(1, NZ)] + [other]
    for peer in peers:
        pl.semaphore_signal(barrier, inc=1, device_id=peer, device_id_type=MESH)
    local = []

    def fetch(src, dst):
        copy = pltpu.make_async_copy(src, dst, local_sem.at[len(local)])
        copy.start()
        local.append(copy)
        return copy

    get_text = [fetch(text_ref, text), fetch(in_gain_hbm, in_gain_ref)]
    get_vis = [fetch(vis_ref.at[:, pl.ds(1024 * h, 1024)], vis.at[z, k, h]) for h in range(4)]
    get_own = [
        fetch(kvw_ref.at[:, pl.ds(pl.multiple_of(z * 256 + k * 128, 128), 128)], wkv.at[c]),
        fetch(qw_ref, wq.at[y]),
        fetch(ow_ref.at[pl.ds(0, 128)], woa.at[x, y]),
        fetch(ow_ref.at[pl.ds(128, 128)], wob.at[y, x]),
        fetch(q_gain_hbm, q_gain_ref),
        fetch(k_gain_hbm, k_gain_ref),
        fetch(seg_hbm, seg_ref),
        fetch(seg_img_hbm, seg_img_ref),
        fetch(slot_hbm, slot_ref),
    ]
    for copy in get_text:
        copy.wait()

    @pl.loop(0, 8)
    def _(block):
        rows = pl.ds(pl.multiple_of(block * 16, 16), 16)
        values = text[rows, :].astype(F32)
        mean_sq = jnp.mean(values * values, axis=-1, keepdims=True)
        values = (values * lax.rsqrt(mean_sq + EPS) * in_gain_ref[...]).astype(BF16)
        for b in range(32):
            hid[b % NX, b // NX // 4, b // NX % 4, rows, :] = values[:, b * 128:(b + 1) * 128]

    for copy in get_vis + get_own:
        copy.wait()
    pl.semaphore_wait(barrier, len(peers))

    vis_p, vis_m, vis_o = {}, {}, []
    kv_y, kv_x = {}, []
    q_p, q_m, a_p, a_m, b_p, b_m = {}, {}, {}, {}, {}, {}
    hid_x, hid_o, b_x, b_x2, a_x, a_x2, o_o = {}, {}, {}, {}, {}, {}, []
    part_x, kv_a, kv_o, heads, upd_z = {}, {}, [], [], {}
    query = []

    def vis_send():
        for h in range(4):
            vis_p[1, h] = send(vis.at[z, k, h], vis.at[z, k, h], to_z(1))
            vis_m[1, h] = send(vis.at[z, k, h], vis.at[z, k, h], to_z(-1))

    def vis_share():
        vis_o.append(send(vis.at[z, k], vis.at[z, k], other))

    def vis_step(s):
        for h in (0, 2, 1, 3):
            for ring, sign in ((vis_p, 1), (vis_m, -1)):
                if (s, h) not in ring:
                    continue
                ring[s, h].wait_recv()
                if s < 3 or (s == 3 and (h < 2) == (sign == 1)):
                    block = vis.at[wrap(z - sign * s, NZ), k, h]
                    ring[s + 1, h] = send(block, block, to_z(sign))
        for sign in ((1, -1) if s < 4 else (1,)):
            block = vis.at[wrap(z - sign * s, NZ), k]
            vis_o.append(send(block, block, other))

    def kv_send():
        for d in (1, -1, 2, -2, 3, -3, 4):
            kv_y[d] = send(wkv.at[c], wkv.at[c], to_y(d))

    def kv_send_x():
        kv_x.extend(send(wkv.at[c], wkv.at[c], to_x(d)) for d in (1, -1, 2))

    def kv_step(s):
        for d in ((s, -s) if s < 4 else (4,)):
            kv_y[d].wait_recv()
            block = wkv.at[wrap(y - d, NY) * NX + x]
            for e in (1, -1, 2):
                kv_x.append(send(block, block, to_x(e)))

    def row_send(p, m, block):
        p[1] = send(block, block, to_y(1))
        m[1] = send(block, block, to_y(-1))

    def row_step(p, m, s, block, half):
        for ring, sign in ((p, 1), (m, -1)):
            ring[s].wait_recv()
            yy = wrap(y - sign * s, NY)
            if s < 4:
                piece = half(yy, 0 if sign == 1 else 1) if s == 3 else block(yy)
                ring[s + 1] = send(piece, piece, to_y(sign))

    def q_send():
        row_send(q_p, q_m, wq.at[y])

    def q_step(s):
        row_step(q_p, q_m, s, lambda yy: wq.at[yy], lambda yy, n: wq.at[yy, pl.ds(64 * n, 64)])

    def a_send():
        row_send(a_p, a_m, woa.at[x, y])

    def a_step(s):
        row_step(
            a_p, a_m, s, lambda yy: woa.at[x, yy], lambda yy, n: woa.at[x, yy, pl.ds(64 * n, 64)]
        )

    def a_send_x():
        for d in (1, -1):
            a_x[d] = send(woa.at[x], woa.at[x], to_x(d))

    def a_step_x():
        for d in (1, -1):
            a_x[d].wait_recv()
        for d in (1, -1):
            piece = woa.at[wrap(x - d, NX), pl.ds(0 if d == 1 else 4, 4)]
            a_x2[d] = send(piece, piece, to_x(d))

    def a_share():
        for copy in a_x2.values():
            copy.wait_recv()
        for e in (0, 1):
            o_o.append(send(woa.at[2 * (1 - k) + e], woa_other.at[e], other))

    def b_share(yy):
        o_o.append(send(wob.at[yy, pl.ds(2 * (1 - k), 2)], wob_other.at[yy], other))

    def b_send_x():
        for d in (1, -1):
            b_x[d] = send(wob.at[y, x], wob.at[y, x], to_x(d))

    def b_step_x():
        for d in (1, -1):
            b_x[d].wait_recv()
        for d in (1, -1):
            half = wob.at[y, wrap(x - d, NX), pl.ds(0 if d == 1 else 64, 64)]
            b_x2[d] = send(half, half, to_x(d))

    def b_send():
        for copy in b_x2.values():
            copy.wait_recv()
        row_send(b_p, b_m, wob.at[y])
        b_share(y)

    def b_step(s):
        row_step(b_p, b_m, s, lambda yy: wob.at[yy], lambda yy, n: wob.at[yy, pl.ds(2 * n, 2)])
        for d in ((s, -s) if s < 4 else (4,)):
            b_share(wrap(y - d, NY))

    def hid_send():
        for d in (1, 3, 2):
            hid_x[d] = send(hid.at[wrap(x + d, NX), k], hid_in.at[d - 1, k], to_x(d))

    def hid_share():
        for d in (1, 3, 2):
            hid_x[d].wait_recv()
            hid_o[d] = send(hid_in.at[d - 1, k], hid_in.at[d - 1, k], other)

    def make_rows():
        for copy in kv_x + vis_o:
            copy.wait_recv()
        rows = jnp.zeros((256, 128), F32)
        for h in range(4):
            rows += jnp.dot(
                vis[:, :, h].reshape(256, 1024), wkv[8 * h:8 * (h + 1)].reshape(1024, 128),
                preferred_element_type=F32,
            )
        mean_sq = jnp.mean(rows * rows, axis=-1, keepdims=True)
        normed = rows * lax.rsqrt(mean_sq + EPS) * k_gain_ref[...]
        kv_rows[...] = jnp.where(k == 0, normed, rows).reshape(32, 8, 128)

    def pick(block):
        tiles = []
        for s in range(8):
            slot = slot_ref[0, seg_img_ref[s % 2, block * 4 + s // 2]]
            tiles.append(kv_rows[slot])
        return jnp.concatenate(tiles, axis=0).astype(BF16)

    def rows_send():
        for dy in (4, 3, 5, 2, 6, 1, 7, 0):
            for dx in (2, 1, 3, 0):
                n = dy * NX + dx
                if n == 0:
                    kv_all[k, 0] = pick(c)
                    continue
                xx, yy = wrap(x + dx, NX), wrap(y + dy, NY)
                stage[n] = pick(yy * NX + xx)
                kv_a[n] = send(stage.at[n], kv_all.at[k, n], at(xx, yy, z, k))

    def rows_share():
        for dy in (1, 7, 2, 6, 3, 5, 4, 0):
            for dx in range(NX):
                if (dx, dy) != (0, 0):
                    kv_a[dy * NX + dx].wait_recv()
            block = kv_all.at[k, pl.ds(dy * NX, NX)]
            kv_o.append(send(block, block, other))

    def part_send():
        for copy in hid_o.values():
            copy.wait_recv()
        wq_all = wq[...].reshape(1024, 256)
        for d in (1, 3, 2, 0):
            blocks = [
                (hid[x, b // 4, b % 4] if d == 0 else hid_in[d - 1, b // 4, b % 4]) for b in range(8)
            ]
            product = jnp.dot(jnp.concatenate(blocks, axis=1), wq_all, preferred_element_type=F32)
            if d == 0:
                query.append(product)
            else:
                part[d - 1] = product.astype(BF16)
                part_x[d] = send(part.at[d - 1], part_in.at[d - 1], to_x(-d))

    def make_query():
        total = query[0]
        for d in (1, 3, 2):
            part_x[d].wait_recv()
            total += part_in[d - 1].astype(F32)
        for n in (0, 1):
            head = total[:, 128 * n:128 * (n + 1)]
            mean_sq = jnp.mean(head * head, axis=-1, keepdims=True)
            heads.append((head * lax.rsqrt(mean_sq + EPS) * q_gain_ref[...]).astype(BF16))

    def attend():
        for copy in kv_o:
            copy.wait_recv()
        keys = kv_all[0].reshape(2048, 128)
        values = kv_all[1].reshape(2048, 128)
        column = lax.broadcasted_iota(jnp.int32, (128, 2048), 1)
        segment = jnp.transpose(jnp.broadcast_to((seg_ref[...] - 4 * c).astype(F32), (128, 128)))
        live = (lax.rem(column, 64) // 16).astype(F32) == segment[:, :1]
        for n in (0, 1):
            scores = lax.dot_general(
                heads[n], keys, (((1,), (1,)), ((), ())), preferred_element_type=F32
            ) * (128 ** -0.5)
            scores = jnp.where(live, scores, NEG)
            weights = jnp.exp(scores - jnp.max(scores, axis=-1, keepdims=True))
            total = jnp.sum(weights, axis=-1, keepdims=True)
            acc = jnp.dot(weights.astype(BF16), values, preferred_element_type=F32)
            ctx[k, :, 128 * n:128 * (n + 1)] = (acc / total).astype(BF16)
        o_o.append(send(ctx.at[k], ctx.at[k], other))

    def project():
        for copy in o_o:
            copy.wait_recv()
        mine, theirs = ctx[k], ctx[1 - k]

        def product(d):
            zz = wrap(z + d, NZ)
            own_a = jnp.concatenate([woa[2 * k + e, zz] for e in (0, 1)], axis=1)
            own_b = jnp.concatenate([wob[zz, 2 * k + e] for e in (0, 1)], axis=1)
            own_w = jnp.concatenate([own_a, own_b], axis=0)
            other_a = jnp.concatenate([woa_other[e, zz] for e in (0, 1)], axis=1)
            other_b = jnp.concatenate([wob_other[zz, e] for e in (0, 1)], axis=1)
            other_w = jnp.concatenate([other_a, other_b], axis=0)
            total = jnp.dot(mine, own_w, preferred_element_type=F32)
            return total + jnp.dot(theirs, other_w, preferred_element_type=F32)

        rows_of = {1: pl.ds(0, 64), -1: pl.ds(64, 64)}
        upd[3] = product(4).astype(BF16)
        for sign in (1, -1):
            upd_z[4 * sign] = send(upd.at[3, rows_of[sign]], upd_in.at[3, rows_of[sign]], to_z(2 * sign))
        for n, sign in ((4, 1), (5, -1)):
            upd[n] = product(3 * sign).astype(BF16)
            upd_z[3 * sign] = send(upd.at[n], upd_in.at[n], to_z(sign))
        for n, sign in ((0, 1), (1, -1)):
            upd[n] = product(sign).astype(BF16)
            upd_z[sign] = send(upd.at[n], upd_in.at[n], to_z(sign))
        two = {sign: product(2 * sign) for sign in (1, -1)}
        update = product(0).astype(BF16).astype(F32)
        for n, sign in ((2, 1), (6, -1)):
            upd_z[3 * sign].wait_recv()
            upd_z[4 * sign].wait_recv()
            total = two[sign] + upd_in[4 if sign == 1 else 5].astype(F32)
            upd[n] = total.astype(BF16)
            part_rows = rows_of[sign]
            first = 0 if sign == 1 else 64
            upd[n, part_rows] = (total[first:first + 64] + upd_in[3, part_rows].astype(F32)).astype(BF16)
            upd_z[2 * sign] = send(upd.at[n], upd_in.at[n], to_z(2 * sign))
        for n, d in ((0, 1), (1, -1), (2, 2), (6, -2)):
            upd_z[d].wait_recv()
            update += upd_in[n].astype(F32)
        own_text = text[:, pl.ds(pl.multiple_of(i * 256, 256), 256)].astype(F32)
        gate = jnp.tanh(jnp.full((1, 256), gate_ref[0], F32))
        out_ref[...] = (own_text + gate * update).astype(BF16)

    vis_send()
    kv_send()
    kv_send_x()
    vis_share()
    q_send()
    a_send()
    b_send_x()
    vis_step(1)
    b_step_x()
    kv_step(1)
    q_step(1)
    a_step(1)
    vis_step(2)
    kv_step(2)
    b_send()
    kv_step(3)
    kv_step(4)
    q_step(2)
    a_step(2)
    vis_step(3)
    hid_send()
    b_step(1)
    q_step(3)
    a_step(3)
    vis_step(4)
    make_rows()
    rows_send()
    b_step(2)
    a_step(4)
    a_send_x()
    hid_share()
    q_step(4)
    part_send()
    b_step(3)
    make_query()
    a_step_x()
    b_step(4)
    rows_share()
    attend()
    a_share()
    project()
    for copy in sent:
        copy.wait_send()


def body(
    text, input_gain, q_weight, kv_weight, o_weight, q_gain, k_gain, attn_gate, vision, segment_ids,
    seg_images, image_slot,
):
    vmem = pl.BlockSpec(memory_space=pltpu.VMEM)
    smem = pl.BlockSpec(memory_space=pltpu.SMEM)
    hbm = pl.BlockSpec(memory_space=pltpu.HBM)
    return pl.pallas_call(
        kernel,
        out_shape=jax.ShapeDtypeStruct((128, 256), BF16),
        in_specs=[hbm] * 7 + [smem] + [hbm] * 4,
        out_specs=vmem,
        scratch_shapes=[
            pltpu.VMEM((1, 4096), F32),
            pltpu.VMEM((1, 128), F32),
            pltpu.VMEM((1, 128), F32),
            pltpu.VMEM((1, 128), jnp.int32),
            pltpu.SMEM((2, 128), jnp.int32),
            pltpu.SMEM((1, 32), jnp.int32),
            pltpu.VMEM((128, 4096), BF16),
            pltpu.VMEM((4, 2, 4, 128, 128), BF16),
            pltpu.VMEM((3, 2, 4, 128, 128), BF16),
            pltpu.VMEM((8, 2, 4, 16, 1024), BF16),
            pltpu.VMEM((32, 128, 128), BF16),
            pltpu.VMEM((8, 128, 256), BF16),
            pltpu.VMEM((4, 8, 128, 128), BF16),
            pltpu.VMEM((8, 4, 128, 128), BF16),
            pltpu.VMEM((2, 8, 128, 128), BF16),
            pltpu.VMEM((8, 2, 128, 128), BF16),
            pltpu.VMEM((3, 128, 256), BF16),
            pltpu.VMEM((3, 128, 256), BF16),
            pltpu.VMEM((32, 8, 128), F32),
            pltpu.VMEM((32, 64, 128), BF16),
            pltpu.VMEM((2, 32, 64, 128), BF16),
            pltpu.VMEM((2, 128, 256), BF16),
            pltpu.VMEM((7, 128, 256), BF16),
            pltpu.VMEM((7, 128, 256), BF16),
            pltpu.SemaphoreType.DMA((COPIES,)),
            pltpu.SemaphoreType.DMA((COPIES,)),
            pltpu.SemaphoreType.DMA((32,)),
        ],
        compiler_params=pltpu.CompilerParams(
            collective_id=0, has_side_effects=True, vmem_limit_bytes=67 * 10**6
        ),
        cost_estimate=pl.CostEstimate(flops=2 * 10**9, bytes_accessed=4 * 10**6, transcendentals=600000),
    )(
        text, input_gain.reshape(1, -1), q_weight, kv_weight, o_weight, q_gain.reshape(1, -1),
        k_gain.reshape(1, -1), attn_gate, vision.reshape(16, 4096), segment_ids.reshape(1, -1),
        seg_images.T, image_slot.reshape(1, -1),
    )


def solution(mesh):
    return jax.shard_map(
        body,
        mesh=mesh,
        in_specs=(
            P("ctx", None), P(), P("ctx", "img"), P("ctx", None), P("img", "ctx"), P(), P(), P(),
            P("img", "ctx", None), P("ctx"), P(), P(),
        ),
        out_specs=P("ctx", "img"),
        check_vma=False,
    )
```

```python
import functools

import jax
import jax.numpy as jnp
from jax import lax
from jax.experimental import pallas as pl
from jax.experimental.pallas import tpu as pltpu
from jax.sharding import PartitionSpec as P

MESH = pl.DeviceIdType.MESH
EPS = 1e-05
NEG = -1e30
F32 = jnp.float32
BF16 = jnp.bfloat16
NX, NY, NZ = 4, 8, 8
COPIES = 192


def kernel(
    text_ref, in_gain_hbm, qw_ref, kvw_ref, ow_ref, q_gain_hbm, k_gain_hbm, gate_ref, vis_ref,
    seg_hbm, seg_img_hbm, slot_hbm, out_ref,
    in_gain_ref, q_gain_ref, k_gain_ref, seg_ref, seg_img_ref, slot_ref, text, hid, hid_in, vis, wkv, wq, woa, wob, woa_other, wob_other, part, part_in, kv_rows, stage, kv_all, ctx, upd, upd_in,
    send_sem, recv_sem, local_sem,
):
    c = lax.axis_index("ctx")
    i = lax.axis_index("img")
    x, y, z, k = lax.rem(c, NX), c // NX, i // 2, lax.rem(i, 2)
    wrap = lambda a, n: lax.rem(a + 2 * n, n)
    at = lambda xx, yy, zz, kk: (yy * NX + xx, zz * 2 + kk)
    to_x = lambda d: at(wrap(x + d, NX), y, z, k)
    to_y = lambda d: at(x, wrap(y + d, NY), z, k)
    to_z = lambda d: at(x, y, wrap(z + d, NZ), k)
    other = at(x, y, z, 1 - k)
    sent = []

    def send(src, dst, device):
        n = len(sent)
        copy = pltpu.make_async_remote_copy(
            src_ref=src, dst_ref=dst, send_sem=send_sem.at[n], recv_sem=recv_sem.at[n],
            device_id=device, device_id_type=MESH,
        )
        copy.start()
        sent.append(copy)
        return copy

    barrier = pltpu.get_barrier_semaphore()
    peers = [to_x(d) for d in (1, 2, 3)] + [to_y(d) for d in range(1, NY)]
    peers += [to_z(d) for d in range(1, NZ)] + [other]
    for peer in peers:
        pl.semaphore_signal(barrier, inc=1, device_id=peer, device_id_type=MESH)
    local = []

    def fetch(src, dst):
        copy = pltpu.make_async_copy(src, dst, local_sem.at[len(local)])
        copy.start()
        local.append(copy)
        return copy

    get_text = [fetch(text_ref, text), fetch(in_gain_hbm, in_gain_ref)]
    get_vis = [fetch(vis_ref.at[:, pl.ds(1024 * h, 1024)], vis.at[z, k, h]) for h in range(4)]
    get_own = [
        fetch(kvw_ref.at[:, pl.ds(pl.multiple_of(z * 256 + k * 128, 128), 128)], wkv.at[c]),
        fetch(qw_ref, wq.at[y]),
        fetch(ow_ref.at[pl.ds(0, 128)], woa.at[x, y]),
        fetch(ow_ref.at[pl.ds(128, 128)], wob.at[y, x]),
        fetch(q_gain_hbm, q_gain_ref),
        fetch(k_gain_hbm, k_gain_ref),
        fetch(seg_hbm, seg_ref),
        fetch(seg_img_hbm, seg_img_ref),
        fetch(slot_hbm, slot_ref),
    ]
    for copy in get_text:
        copy.wait()

    @pl.loop(0, 8)
    def _(block):
        rows = pl.ds(pl.multiple_of(block * 16, 16), 16)
        values = text[rows, :].astype(F32)
        mean_sq = jnp.mean(values * values, axis=-1, keepdims=True)
        values = (values * lax.rsqrt(mean_sq + EPS) * in_gain_ref[...]).astype(BF16)
        for b in range(32):
            hid[b % NX, b // NX // 4, b // NX % 4, rows, :] = values[:, b * 128:(b + 1) * 128]

    for copy in get_vis + get_own:
        copy.wait()
    pl.semaphore_wait(barrier, len(peers))

    vis_p, vis_m, vis_o = {}, {}, []
    kv_y, kv_x = {}, []
    q_p, q_m, a_p, a_m, b_p, b_m = {}, {}, {}, {}, {}, {}
    hid_x, hid_o, b_x, b_x2, a_x, a_x2, o_o = {}, {}, {}, {}, {}, {}, []
    part_x, kv_a, kv_o, heads, upd_z = {}, {}, [], [], {}
    query = []

    def vis_send():
        for h in range(4):
            vis_p[1, h] = send(vis.at[z, k, h], vis.at[z, k, h], to_z(1))
            vis_m[1, h] = send(vis.at[z, k, h], vis.at[z, k, h], to_z(-1))

    def vis_share():
        vis_o.append(send(vis.at[z, k], vis.at[z, k], other))

    def vis_step(s):
        for h in (0, 2, 1, 3):
            for ring, sign in ((vis_p, 1), (vis_m, -1)):
                if (s, h) not in ring:
                    continue
                ring[s, h].wait_recv()
                if s < 3 or (s == 3 and (h < 2) == (sign == 1)):
                    block = vis.at[wrap(z - sign * s, NZ), k, h]
                    ring[s + 1, h] = send(block, block, to_z(sign))
        for sign in ((1, -1) if s < 4 else (1,)):
            block = vis.at[wrap(z - sign * s, NZ), k]
            vis_o.append(send(block, block, other))

    def kv_send():
        for d in (1, -1, 2, -2, 3, -3, 4):
            kv_y[d] = send(wkv.at[c], wkv.at[c], to_y(d))

    def kv_send_x():
        kv_x.extend(send(wkv.at[c], wkv.at[c], to_x(d)) for d in (1, -1, 2))

    def kv_step(s):
        for d in ((s, -s) if s < 4 else (4,)):
            kv_y[d].wait_recv()
            block = wkv.at[wrap(y - d, NY) * NX + x]
            for e in (1, -1, 2):
                kv_x.append(send(block, block, to_x(e)))

    def row_send(p, m, block):
        p[1] = send(block, block, to_y(1))
        m[1] = send(block, block, to_y(-1))

    def row_step(p, m, s, block, half):
        for ring, sign in ((p, 1), (m, -1)):
            ring[s].wait_recv()
            yy = wrap(y - sign * s, NY)
            if s < 4:
                piece = half(yy, 0 if sign == 1 else 1) if s == 3 else block(yy)
                ring[s + 1] = send(piece, piece, to_y(sign))

    def q_send():
        row_send(q_p, q_m, wq.at[y])

    def q_step(s):
        row_step(q_p, q_m, s, lambda yy: wq.at[yy], lambda yy, n: wq.at[yy, pl.ds(64 * n, 64)])

    def a_send():
        row_send(a_p, a_m, woa.at[x, y])

    def a_step(s):
        row_step(
            a_p, a_m, s, lambda yy: woa.at[x, yy], lambda yy, n: woa.at[x, yy, pl.ds(64 * n, 64)]
        )

    def a_send_x():
        for d in (1, -1):
            a_x[d] = send(woa.at[x], woa.at[x], to_x(d))

    near = jnp.where(x // 2 == 1 - k, lax.rem(x, 2), 1 - lax.rem(x, 2))

    def a_pass(e):
        o_o.append(send(woa.at[2 * (1 - k) + e], woa_other.at[e], other))

    def a_step_x():
        for d in (1, -1):
            a_x[d].wait_recv()
        for d in (1, -1):
            piece = woa.at[wrap(x - d, NX), pl.ds(0 if d == 1 else 4, 4)]
            a_x2[d] = send(piece, piece, to_x(d))
        a_pass(near)

    def a_share():
        for copy in a_x2.values():
            copy.wait_recv()
        a_pass(1 - near)

    def b_share(yy):
        o_o.append(send(wob.at[yy, pl.ds(2 * (1 - k), 2)], wob_other.at[yy], other))

    def b_send_x():
        for d in (1, -1):
            b_x[d] = send(wob.at[y, x], wob.at[y, x], to_x(d))

    def b_step_x():
        for d in (1, -1):
            b_x[d].wait_recv()
        for d in (1, -1):
            half = wob.at[y, wrap(x - d, NX), pl.ds(0 if d == 1 else 64, 64)]
            b_x2[d] = send(half, half, to_x(d))

    def b_send():
        for copy in b_x2.values():
            copy.wait_recv()
        row_send(b_p, b_m, wob.at[y])
        b_share(y)

    def b_step(s):
        row_step(b_p, b_m, s, lambda yy: wob.at[yy], lambda yy, n: wob.at[yy, pl.ds(2 * n, 2)])
        for d in ((s, -s) if s < 4 else (4,)):
            b_share(wrap(y - d, NY))

    def hid_send():
        for d in (1, 3, 2):
            hid_x[d] = send(hid.at[wrap(x + d, NX), k], hid_in.at[d - 1, k], to_x(d))

    def hid_share():
        for d in (1, 3, 2):
            hid_x[d].wait_recv()
            hid_o[d] = send(hid_in.at[d - 1, k], hid_in.at[d - 1, k], other)

    def make_rows():
        for copy in kv_x + vis_o:
            copy.wait_recv()
        rows = jnp.zeros((256, 128), F32)
        for h in range(4):
            rows += jnp.dot(
                vis[:, :, h].reshape(256, 1024), wkv[8 * h:8 * (h + 1)].reshape(1024, 128),
                preferred_element_type=F32,
            )
        mean_sq = jnp.mean(rows * rows, axis=-1, keepdims=True)
        normed = rows * lax.rsqrt(mean_sq + EPS) * k_gain_ref[...]
        kv_rows[...] = jnp.where(k == 0, normed, rows).reshape(32, 8, 128)

    def pick(block):
        tiles = []
        for s in range(8):
            slot = slot_ref[0, seg_img_ref[s % 2, block * 4 + s // 2]]
            tiles.append(kv_rows[slot])
        return jnp.concatenate(tiles, axis=0).astype(BF16)

    def rows_send():
        for dy in (4, 3, 5, 2, 6, 1, 7, 0):
            for dx in (2, 1, 3, 0):
                n = dy * NX + dx
                if n == 0:
                    kv_all[k, 0] = pick(c)
                    continue
                xx, yy = wrap(x + dx, NX), wrap(y + dy, NY)
                stage[n] = pick(yy * NX + xx)
                kv_a[n] = send(stage.at[n], kv_all.at[k, n], at(xx, yy, z, k))

    def rows_share():
        for dy in (1, 7, 2, 6, 3, 5, 4, 0):
            for dx in range(NX):
                if (dx, dy) != (0, 0):
                    kv_a[dy * NX + dx].wait_recv()
            block = kv_all.at[k, pl.ds(dy * NX, NX)]
            kv_o.append(send(block, block, other))

    def part_send():
        for copy in hid_o.values():
            copy.wait_recv()
        wq_all = wq[...].reshape(1024, 256)
        for d in (1, 3, 2, 0):
            blocks = [
                (hid[x, b // 4, b % 4] if d == 0 else hid_in[d - 1, b // 4, b % 4]) for b in range(8)
            ]
            product = jnp.dot(jnp.concatenate(blocks, axis=1), wq_all, preferred_element_type=F32)
            if d == 0:
                query.append(product)
            else:
                part[d - 1] = product.astype(BF16)
                part_x[d] = send(part.at[d - 1], part_in.at[d - 1], to_x(-d))

    def make_query():
        total = query[0]
        for d in (1, 3, 2):
            part_x[d].wait_recv()
            total += part_in[d - 1].astype(F32)
        for n in (0, 1):
            head = total[:, 128 * n:128 * (n + 1)]
            mean_sq = jnp.mean(head * head, axis=-1, keepdims=True)
            heads.append((head * lax.rsqrt(mean_sq + EPS) * q_gain_ref[...]).astype(BF16))

    def attend():
        for copy in kv_o:
            copy.wait_recv()
        keys = kv_all[0].reshape(2048, 128)
        values = kv_all[1].reshape(2048, 128)
        column = lax.broadcasted_iota(jnp.int32, (128, 2048), 1)
        segment = jnp.transpose(jnp.broadcast_to((seg_ref[...] - 4 * c).astype(F32), (128, 128)))
        live = (lax.rem(column, 64) // 16).astype(F32) == segment[:, :1]
        for n in (0, 1):
            scores = lax.dot_general(
                heads[n], keys, (((1,), (1,)), ((), ())), preferred_element_type=F32
            ) * (128 ** -0.5)
            scores = jnp.where(live, scores, NEG)
            weights = jnp.exp(scores - jnp.max(scores, axis=-1, keepdims=True))
            total = jnp.sum(weights, axis=-1, keepdims=True)
            acc = jnp.dot(weights.astype(BF16), values, preferred_element_type=F32)
            ctx[k, n] = (acc / total).astype(BF16)
            o_o.append(send(ctx.at[k, n], ctx.at[k, n], other))

    def project():
        for copy in o_o:
            copy.wait_recv()
        mine, theirs = (jnp.concatenate([ctx[m, n] for n in (0, 1)], axis=1) for m in (k, 1 - k))

        def product(d):
            zz = wrap(z + d, NZ)
            own_a = jnp.concatenate([woa[2 * k + e, zz] for e in (0, 1)], axis=1)
            own_b = jnp.concatenate([wob[zz, 2 * k + e] for e in (0, 1)], axis=1)
            own_w = jnp.concatenate([own_a, own_b], axis=0)
            other_a = jnp.concatenate([woa_other[e, zz] for e in (0, 1)], axis=1)
            other_b = jnp.concatenate([wob_other[zz, e] for e in (0, 1)], axis=1)
            other_w = jnp.concatenate([other_a, other_b], axis=0)
            total = jnp.dot(mine, own_w, preferred_element_type=F32)
            return total + jnp.dot(theirs, other_w, preferred_element_type=F32)

        rows_of = {1: pl.ds(0, 64), -1: pl.ds(64, 64)}
        upd[3] = product(4).astype(BF16)
        for sign in (1, -1):
            upd_z[4 * sign] = send(upd.at[3, rows_of[sign]], upd_in.at[3, rows_of[sign]], to_z(2 * sign))
        for n, sign in ((4, 1), (5, -1)):
            upd[n] = product(3 * sign).astype(BF16)
            upd_z[3 * sign] = send(upd.at[n], upd_in.at[n], to_z(sign))
        for n, sign in ((0, 1), (1, -1)):
            upd[n] = product(sign).astype(BF16)
            upd_z[sign] = send(upd.at[n], upd_in.at[n], to_z(sign))
        two = {sign: product(2 * sign) for sign in (1, -1)}
        update = product(0).astype(BF16).astype(F32)
        for n, sign in ((2, 1), (6, -1)):
            upd_z[3 * sign].wait_recv()
            upd_z[4 * sign].wait_recv()
            total = two[sign] + upd_in[4 if sign == 1 else 5].astype(F32)
            upd[n] = total.astype(BF16)
            part_rows = rows_of[sign]
            first = 0 if sign == 1 else 64
            upd[n, part_rows] = (total[first:first + 64] + upd_in[3, part_rows].astype(F32)).astype(BF16)
            upd_z[2 * sign] = send(upd.at[n], upd_in.at[n], to_z(2 * sign))
        for n, d in ((0, 1), (1, -1), (2, 2), (6, -2)):
            upd_z[d].wait_recv()
            update += upd_in[n].astype(F32)
        own_text = text[:, pl.ds(pl.multiple_of(i * 256, 256), 256)].astype(F32)
        gate = jnp.tanh(jnp.full((1, 256), gate_ref[0], F32))
        out_ref[...] = (own_text + gate * update).astype(BF16)

    vis_send()
    kv_send()
    kv_send_x()
    vis_share()
    q_send()
    a_send()
    b_send_x()
    vis_step(1)
    b_step_x()
    kv_step(1)
    q_step(1)
    a_step(1)
    vis_step(2)
    kv_step(2)
    b_send()
    kv_step(3)
    kv_step(4)
    q_step(2)
    a_step(2)
    vis_step(3)
    hid_send()
    b_step(1)
    q_step(3)
    a_step(3)
    vis_step(4)
    make_rows()
    rows_send()
    a_step(4)
    a_send_x()
    b_step(2)
    hid_share()
    q_step(4)
    part_send()
    a_step_x()
    b_step(3)
    make_query()
    rows_share()
    attend()
    b_step(4)
    a_share()
    project()
    for copy in sent:
        copy.wait_send()


def body(
    text, input_gain, q_weight, kv_weight, o_weight, q_gain, k_gain, attn_gate, vision, segment_ids,
    seg_images, image_slot,
):
    vmem = pl.BlockSpec(memory_space=pltpu.VMEM)
    smem = pl.BlockSpec(memory_space=pltpu.SMEM)
    hbm = pl.BlockSpec(memory_space=pltpu.HBM)
    return pl.pallas_call(
        kernel,
        out_shape=jax.ShapeDtypeStruct((128, 256), BF16),
        in_specs=[hbm] * 7 + [smem] + [hbm] * 4,
        out_specs=vmem,
        scratch_shapes=[
            pltpu.VMEM((1, 4096), F32),
            pltpu.VMEM((1, 128), F32),
            pltpu.VMEM((1, 128), F32),
            pltpu.VMEM((1, 128), jnp.int32),
            pltpu.SMEM((2, 128), jnp.int32),
            pltpu.SMEM((1, 32), jnp.int32),
            pltpu.VMEM((128, 4096), BF16),
            pltpu.VMEM((4, 2, 4, 128, 128), BF16),
            pltpu.VMEM((3, 2, 4, 128, 128), BF16),
            pltpu.VMEM((8, 2, 4, 16, 1024), BF16),
            pltpu.VMEM((32, 128, 128), BF16),
            pltpu.VMEM((8, 128, 256), BF16),
            pltpu.VMEM((4, 8, 128, 128), BF16),
            pltpu.VMEM((8, 4, 128, 128), BF16),
            pltpu.VMEM((2, 8, 128, 128), BF16),
            pltpu.VMEM((8, 2, 128, 128), BF16),
            pltpu.VMEM((3, 128, 256), BF16),
            pltpu.VMEM((3, 128, 256), BF16),
            pltpu.VMEM((32, 8, 128), F32),
            pltpu.VMEM((32, 64, 128), BF16),
            pltpu.VMEM((2, 32, 64, 128), BF16),
            pltpu.VMEM((2, 2, 128, 128), BF16),
            pltpu.VMEM((7, 128, 256), BF16),
            pltpu.VMEM((7, 128, 256), BF16),
            pltpu.SemaphoreType.DMA((COPIES,)),
            pltpu.SemaphoreType.DMA((COPIES,)),
            pltpu.SemaphoreType.DMA((32,)),
        ],
        compiler_params=pltpu.CompilerParams(
            collective_id=0, has_side_effects=True, vmem_limit_bytes=67 * 10**6
        ),
        cost_estimate=pl.CostEstimate(flops=2 * 10**9, bytes_accessed=4 * 10**6, transcendentals=600000),
    )(
        text, input_gain.reshape(1, -1), q_weight, kv_weight, o_weight, q_gain.reshape(1, -1),
        k_gain.reshape(1, -1), attn_gate, vision.reshape(16, 4096), segment_ids.reshape(1, -1),
        seg_images.T, image_slot.reshape(1, -1),
    )


def solution(mesh):
    return jax.shard_map(
        body,
        mesh=mesh,
        in_specs=(
            P("ctx", None), P(), P("ctx", "img"), P("ctx", None), P("img", "ctx"), P(), P(), P(),
            P("img", "ctx", None), P("ctx"), P(), P(),
        ),
        out_specs=P("ctx", "img"),
        check_vma=False,
    )
```

```python
import functools

import jax
import jax.numpy as jnp
from jax import lax
from jax.experimental import pallas as pl
from jax.experimental.pallas import tpu as pltpu
from jax.sharding import PartitionSpec as P

MESH = pl.DeviceIdType.MESH
EPS = 1e-05
NEG = -1e30
F32 = jnp.float32
BF16 = jnp.bfloat16
NX, NY, NZ = 4, 8, 8
COPIES = 192


def kernel(
    text_ref, in_gain_hbm, qw_ref, kvw_ref, ow_ref, q_gain_hbm, k_gain_hbm, gate_ref, vis_ref,
    seg_hbm, seg_img_hbm, slot_hbm, out_ref,
    in_gain_ref, q_gain_ref, k_gain_ref, seg_ref, seg_img_ref, slot_ref, text, hid, hid_in, vis, wkv, wq, woa, wob, woa_other, wob_other, part, part_in, kv_rows, stage, kv_all, ctx, upd, upd_in,
    send_sem, recv_sem, local_sem,
):
    c = lax.axis_index("ctx")
    i = lax.axis_index("img")
    x, y, z, k = lax.rem(c, NX), c // NX, i // 2, lax.rem(i, 2)
    wrap = lambda a, n: lax.rem(a + 2 * n, n)
    at = lambda xx, yy, zz, kk: (yy * NX + xx, zz * 2 + kk)
    to_x = lambda d: at(wrap(x + d, NX), y, z, k)
    to_y = lambda d: at(x, wrap(y + d, NY), z, k)
    to_z = lambda d: at(x, y, wrap(z + d, NZ), k)
    other = at(x, y, z, 1 - k)
    sent = []

    def send(src, dst, device):
        n = len(sent)
        copy = pltpu.make_async_remote_copy(
            src_ref=src, dst_ref=dst, send_sem=send_sem.at[n], recv_sem=recv_sem.at[n],
            device_id=device, device_id_type=MESH,
        )
        copy.start()
        sent.append(copy)
        return copy

    barrier = pltpu.get_barrier_semaphore()
    peers = [to_x(d) for d in (1, 2, 3)] + [to_y(d) for d in range(1, NY)]
    peers += [to_z(d) for d in range(1, NZ)] + [other]
    for peer in peers:
        pl.semaphore_signal(barrier, inc=1, device_id=peer, device_id_type=MESH)
    local = []

    def fetch(src, dst):
        copy = pltpu.make_async_copy(src, dst, local_sem.at[len(local)])
        copy.start()
        local.append(copy)
        return copy

    get_text = [fetch(text_ref, text), fetch(in_gain_hbm, in_gain_ref)]
    get_vis = [fetch(vis_ref.at[:, pl.ds(1024 * h, 1024)], vis.at[z, k, h]) for h in range(4)]
    get_own = [
        fetch(kvw_ref.at[:, pl.ds(pl.multiple_of(z * 256 + k * 128, 128), 128)], wkv.at[c]),
        fetch(qw_ref, wq.at[y]),
        fetch(ow_ref.at[pl.ds(0, 128)], woa.at[x, y]),
        fetch(ow_ref.at[pl.ds(128, 128)], wob.at[y, x]),
        fetch(q_gain_hbm, q_gain_ref),
        fetch(k_gain_hbm, k_gain_ref),
        fetch(seg_hbm, seg_ref),
        fetch(seg_img_hbm, seg_img_ref),
        fetch(slot_hbm, slot_ref),
    ]
    for copy in get_text:
        copy.wait()

    @pl.loop(0, 8)
    def _(block):
        rows = pl.ds(pl.multiple_of(block * 16, 16), 16)
        values = text[rows, :].astype(F32)
        mean_sq = jnp.mean(values * values, axis=-1, keepdims=True)
        values = (values * lax.rsqrt(mean_sq + EPS) * in_gain_ref[...]).astype(BF16)
        for b in range(32):
            hid[b % NX, b // NX // 4, b // NX % 4, rows, :] = values[:, b * 128:(b + 1) * 128]

    for copy in get_vis + get_own:
        copy.wait()
    pl.semaphore_wait(barrier, len(peers))

    vis_p, vis_m, vis_o = {}, {}, []
    kv_y, kv_x = {}, []
    q_p, q_m, a_p, a_m, b_p, b_m = {}, {}, {}, {}, {}, {}
    hid_x, hid_o, b_x, b_x2, a_x, a_x2, o_o = {}, {}, {}, {}, {}, {}, []
    part_x, kv_a, kv_o, heads, upd_z = {}, {}, [], [], {}
    query = []

    def vis_send():
        for h in range(4):
            vis_p[1, h] = send(vis.at[z, k, h], vis.at[z, k, h], to_z(1))
            vis_m[1, h] = send(vis.at[z, k, h], vis.at[z, k, h], to_z(-1))

    def vis_share():
        vis_o.append(send(vis.at[z, k], vis.at[z, k], other))

    def vis_step(s):
        for h in (0, 2, 1, 3):
            for ring, sign in ((vis_p, 1), (vis_m, -1)):
                if (s, h) not in ring:
                    continue
                ring[s, h].wait_recv()
                if s == 4:
                    block = vis.at[wrap(z + 4, NZ), k, h]
                    vis_o.append(send(block, block, other))
                if s < 3 or (s == 3 and (h < 2) == (sign == 1)):
                    block = vis.at[wrap(z - sign * s, NZ), k, h]
                    ring[s + 1, h] = send(block, block, to_z(sign))
        for sign in ((1, -1) if s < 4 else ()):
            block = vis.at[wrap(z - sign * s, NZ), k]
            vis_o.append(send(block, block, other))

    def kv_send():
        for d in (1, -1, 2, -2, 3, -3, 4):
            kv_y[d] = send(wkv.at[c], wkv.at[c], to_y(d))

    def kv_send_x():
        kv_x.extend(send(wkv.at[c], wkv.at[c], to_x(d)) for d in (1, -1, 2))

    def kv_step(s):
        for d in ((s, -s) if s < 4 else (4,)):
            kv_y[d].wait_recv()
            block = wkv.at[wrap(y - d, NY) * NX + x]
            for e in (1, -1, 2):
                kv_x.append(send(block, block, to_x(e)))

    def row_send(p, m, block):
        p[1] = send(block, block, to_y(1))
        m[1] = send(block, block, to_y(-1))

    def row_step(p, m, s, block, half):
        for ring, sign in ((p, 1), (m, -1)):
            ring[s].wait_recv()
            yy = wrap(y - sign * s, NY)
            if s < 4:
                piece = half(yy, 0 if sign == 1 else 1) if s == 3 else block(yy)
                ring[s + 1] = send(piece, piece, to_y(sign))

    def q_send():
        row_send(q_p, q_m, wq.at[y])

    def q_step(s):
        row_step(q_p, q_m, s, lambda yy: wq.at[yy], lambda yy, n: wq.at[yy, pl.ds(64 * n, 64)])

    def a_send():
        row_send(a_p, a_m, woa.at[x, y])

    def a_step(s):
        row_step(
            a_p, a_m, s, lambda yy: woa.at[x, yy], lambda yy, n: woa.at[x, yy, pl.ds(64 * n, 64)]
        )

    def a_send_x():
        for d in (1, -1):
            a_x[d] = send(woa.at[x], woa.at[x], to_x(d))

    near = jnp.where(x // 2 == 1 - k, lax.rem(x, 2), 1 - lax.rem(x, 2))

    def a_pass(e):
        o_o.append(send(woa.at[2 * (1 - k) + e], woa_other.at[e], other))

    def a_step_x():
        for d in (1, -1):
            a_x[d].wait_recv()
        for d in (1, -1):
            piece = woa.at[wrap(x - d, NX), pl.ds(0 if d == 1 else 4, 4)]
            a_x2[d] = send(piece, piece, to_x(d))
        a_pass(near)

    def a_share():
        for copy in a_x2.values():
            copy.wait_recv()
        a_pass(1 - near)

    def b_share(yy):
        o_o.append(send(wob.at[yy, pl.ds(2 * (1 - k), 2)], wob_other.at[yy], other))

    def b_send_x():
        for d in (1, -1):
            b_x[d] = send(wob.at[y, x], wob.at[y, x], to_x(d))

    def b_step_x():
        for d in (1, -1):
            b_x[d].wait_recv()
        for d in (1, -1):
            half = wob.at[y, wrap(x - d, NX), pl.ds(0 if d == 1 else 64, 64)]
            b_x2[d] = send(half, half, to_x(d))

    def b_send():
        for copy in b_x2.values():
            copy.wait_recv()
        row_send(b_p, b_m, wob.at[y])
        b_share(y)

    def b_step(s):
        row_step(b_p, b_m, s, lambda yy: wob.at[yy], lambda yy, n: wob.at[yy, pl.ds(2 * n, 2)])
        for d in ((s, -s) if s < 4 else (4,)):
            b_share(wrap(y - d, NY))

    def hid_send():
        for d in (1, 3, 2):
            hid_x[d] = send(hid.at[wrap(x + d, NX), k], hid_in.at[d - 1, k], to_x(d))

    def hid_share():
        for d in (1, 3, 2):
            hid_x[d].wait_recv()
            hid_o[d] = send(hid_in.at[d - 1, k], hid_in.at[d - 1, k], other)

    def make_rows():
        for copy in kv_x + vis_o:
            copy.wait_recv()
        rows = jnp.zeros((256, 128), F32)
        for h in range(4):
            rows += jnp.dot(
                vis[:, :, h].reshape(256, 1024), wkv[8 * h:8 * (h + 1)].reshape(1024, 128),
                preferred_element_type=F32,
            )
        mean_sq = jnp.mean(rows * rows, axis=-1, keepdims=True)
        normed = rows * lax.rsqrt(mean_sq + EPS) * k_gain_ref[...]
        kv_rows[...] = jnp.where(k == 0, normed, rows).reshape(32, 8, 128)

    def pick(block):
        tiles = []
        for s in range(8):
            slot = slot_ref[0, seg_img_ref[s % 2, block * 4 + s // 2]]
            tiles.append(kv_rows[slot])
        return jnp.concatenate(tiles, axis=0).astype(BF16)

    def rows_send():
        for dy in (4, 3, 5, 2, 6, 1, 7, 0):
            for dx in (2, 1, 3, 0):
                n = dy * NX + dx
                if n == 0:
                    kv_all[k, 0] = pick(c)
                    continue
                xx, yy = wrap(x + dx, NX), wrap(y + dy, NY)
                stage[n] = pick(yy * NX + xx)
                kv_a[n] = send(stage.at[n], kv_all.at[k, n], at(xx, yy, z, k))

    def rows_share():
        for dy in (1, 7, 2, 6, 3, 5, 4, 0):
            for dx in range(NX):
                if (dx, dy) != (0, 0):
                    kv_a[dy * NX + dx].wait_recv()
            block = kv_all.at[k, pl.ds(dy * NX, NX)]
            kv_o.append(send(block, block, other))

    def part_send():
        for copy in hid_o.values():
            copy.wait_recv()
        wq_all = wq[...].reshape(1024, 256)
        for d in (1, 3, 2, 0):
            blocks = [
                (hid[x, b // 4, b % 4] if d == 0 else hid_in[d - 1, b // 4, b % 4]) for b in range(8)
            ]
            product = jnp.dot(jnp.concatenate(blocks, axis=1), wq_all, preferred_element_type=F32)
            if d == 0:
                query.append(product)
            else:
                part[d - 1] = product.astype(BF16)
                part_x[d] = send(part.at[d - 1], part_in.at[d - 1], to_x(-d))

    def make_query():
        total = query[0]
        for d in (1, 3, 2):
            part_x[d].wait_recv()
            total += part_in[d - 1].astype(F32)
        for n in (0, 1):
            head = total[:, 128 * n:128 * (n + 1)]
            mean_sq = jnp.mean(head * head, axis=-1, keepdims=True)
            heads.append((head * lax.rsqrt(mean_sq + EPS) * q_gain_ref[...]).astype(BF16))

    def attend():
        for copy in kv_o:
            copy.wait_recv()
        keys = kv_all[0].reshape(2048, 128)
        values = kv_all[1].reshape(2048, 128)
        column = lax.broadcasted_iota(jnp.int32, (128, 2048), 1)
        segment = jnp.transpose(jnp.broadcast_to((seg_ref[...] - 4 * c).astype(F32), (128, 128)))
        live = (lax.rem(column, 64) // 16).astype(F32) == segment[:, :1]
        for n in (0, 1):
            scores = lax.dot_general(
                heads[n], keys, (((1,), (1,)), ((), ())), preferred_element_type=F32
            ) * (128 ** -0.5)
            scores = jnp.where(live, scores, NEG)
            weights = jnp.exp(scores - jnp.max(scores, axis=-1, keepdims=True))
            total = jnp.sum(weights, axis=-1, keepdims=True)
            acc = jnp.dot(weights.astype(BF16), values, preferred_element_type=F32)
            ctx[k, n] = (acc / total).astype(BF16)
            o_o.append(send(ctx.at[k, n], ctx.at[k, n], other))

    def project():
        for copy in o_o:
            copy.wait_recv()
        mine, theirs = (jnp.concatenate([ctx[m, n] for n in (0, 1)], axis=1) for m in (k, 1 - k))

        def product(d):
            zz = wrap(z + d, NZ)
            own_a = jnp.concatenate([woa[2 * k + e, zz] for e in (0, 1)], axis=1)
            own_b = jnp.concatenate([wob[zz, 2 * k + e] for e in (0, 1)], axis=1)
            own_w = jnp.concatenate([own_a, own_b], axis=0)
            other_a = jnp.concatenate([woa_other[e, zz] for e in (0, 1)], axis=1)
            other_b = jnp.concatenate([wob_other[zz, e] for e in (0, 1)], axis=1)
            other_w = jnp.concatenate([other_a, other_b], axis=0)
            total = jnp.dot(mine, own_w, preferred_element_type=F32)
            return total + jnp.dot(theirs, other_w, preferred_element_type=F32)

        rows_of = {1: pl.ds(0, 64), -1: pl.ds(64, 64)}
        upd[3] = product(4).astype(BF16)
        for sign in (1, -1):
            upd_z[4 * sign] = send(upd.at[3, rows_of[sign]], upd_in.at[3, rows_of[sign]], to_z(2 * sign))
        for n, sign in ((4, 1), (5, -1)):
            upd[n] = product(3 * sign).astype(BF16)
            upd_z[3 * sign] = send(upd.at[n], upd_in.at[n], to_z(sign))
        for n, sign in ((0, 1), (1, -1)):
            upd[n] = product(sign).astype(BF16)
            upd_z[sign] = send(upd.at[n], upd_in.at[n], to_z(sign))
        two = {sign: product(2 * sign) for sign in (1, -1)}
        update = product(0).astype(BF16).astype(F32)
        for n, sign in ((2, 1), (6, -1)):
            upd_z[3 * sign].wait_recv()
            upd_z[4 * sign].wait_recv()
            total = two[sign] + upd_in[4 if sign == 1 else 5].astype(F32)
            upd[n] = total.astype(BF16)
            part_rows = rows_of[sign]
            first = 0 if sign == 1 else 64
            upd[n, part_rows] = (total[first:first + 64] + upd_in[3, part_rows].astype(F32)).astype(BF16)
            upd_z[2 * sign] = send(upd.at[n], upd_in.at[n], to_z(2 * sign))
        for n, d in ((0, 1), (1, -1), (2, 2), (6, -2)):
            upd_z[d].wait_recv()
            update += upd_in[n].astype(F32)
        own_text = text[:, pl.ds(pl.multiple_of(i * 256, 256), 256)].astype(F32)
        gate = jnp.tanh(jnp.full((1, 256), gate_ref[0], F32))
        out_ref[...] = (own_text + gate * update).astype(BF16)

    vis_send()
    kv_send()
    kv_send_x()
    vis_share()
    q_send()
    a_send()
    b_send_x()
    vis_step(1)
    b_step_x()
    kv_step(1)
    q_step(1)
    a_step(1)
    vis_step(2)
    kv_step(2)
    b_send()
    kv_step(3)
    kv_step(4)
    q_step(2)
    a_step(2)
    vis_step(3)
    hid_send()
    b_step(1)
    q_step(3)
    a_step(3)
    vis_step(4)
    make_rows()
    rows_send()
    a_step(4)
    a_send_x()
    b_step(2)
    hid_share()
    q_step(4)
    part_send()
    a_step_x()
    b_step(3)
    make_query()
    rows_share()
    attend()
    b_step(4)
    a_share()
    project()
    for copy in sent:
        copy.wait_send()


def body(
    text, input_gain, q_weight, kv_weight, o_weight, q_gain, k_gain, attn_gate, vision, segment_ids,
    seg_images, image_slot,
):
    vmem = pl.BlockSpec(memory_space=pltpu.VMEM)
    smem = pl.BlockSpec(memory_space=pltpu.SMEM)
    hbm = pl.BlockSpec(memory_space=pltpu.HBM)
    return pl.pallas_call(
        kernel,
        out_shape=jax.ShapeDtypeStruct((128, 256), BF16),
        in_specs=[hbm] * 7 + [smem] + [hbm] * 4,
        out_specs=vmem,
        scratch_shapes=[
            pltpu.VMEM((1, 4096), F32),
            pltpu.VMEM((1, 128), F32),
            pltpu.VMEM((1, 128), F32),
            pltpu.VMEM((1, 128), jnp.int32),
            pltpu.SMEM((2, 128), jnp.int32),
            pltpu.SMEM((1, 32), jnp.int32),
            pltpu.VMEM((128, 4096), BF16),
            pltpu.VMEM((4, 2, 4, 128, 128), BF16),
            pltpu.VMEM((3, 2, 4, 128, 128), BF16),
            pltpu.VMEM((8, 2, 4, 16, 1024), BF16),
            pltpu.VMEM((32, 128, 128), BF16),
            pltpu.VMEM((8, 128, 256), BF16),
            pltpu.VMEM((4, 8, 128, 128), BF16),
            pltpu.VMEM((8, 4, 128, 128), BF16),
            pltpu.VMEM((2, 8, 128, 128), BF16),
            pltpu.VMEM((8, 2, 128, 128), BF16),
            pltpu.VMEM((3, 128, 256), BF16),
            pltpu.VMEM((3, 128, 256), BF16),
            pltpu.VMEM((32, 8, 128), F32),
            pltpu.VMEM((32, 64, 128), BF16),
            pltpu.VMEM((2, 32, 64, 128), BF16),
            pltpu.VMEM((2, 2, 128, 128), BF16),
            pltpu.VMEM((7, 128, 256), BF16),
            pltpu.VMEM((7, 128, 256), BF16),
            pltpu.SemaphoreType.DMA((COPIES,)),
            pltpu.SemaphoreType.DMA((COPIES,)),
            pltpu.SemaphoreType.DMA((32,)),
        ],
        compiler_params=pltpu.CompilerParams(
            collective_id=0, has_side_effects=True, vmem_limit_bytes=56400000
        ),
        cost_estimate=pl.CostEstimate(flops=2 * 10**9, bytes_accessed=4 * 10**6, transcendentals=600000),
    )(
        text, input_gain.reshape(1, -1), q_weight, kv_weight, o_weight, q_gain.reshape(1, -1),
        k_gain.reshape(1, -1), attn_gate, vision.reshape(16, 4096), segment_ids.reshape(1, -1),
        seg_images.T, image_slot.reshape(1, -1),
    )


def solution(mesh):
    return jax.shard_map(
        body,
        mesh=mesh,
        in_specs=(
            P("ctx", None), P(), P("ctx", "img"), P("ctx", None), P("img", "ctx"), P(), P(), P(),
            P("img", "ctx", None), P("ctx"), P(), P(),
        ),
        out_specs=P("ctx", "img"),
        check_vma=False,
    )
```
